512 devices in a mesh: gx: 8 (over y, core), yz: 32 (over z_lo, x), ta: 2 (over z_hi).
Axes of the slice: x: 4, y: 4, z: 16 (z_hi: 2, z_lo: 8; z = z_hi * 8 + z_lo), core: 2. Of those that a mesh axis runs over, the one named last changes fastest.
Arguments:
- field: float32 [4, 4, 512, 32768], P('ta', None, 'gx', 'yz'), may hold values from -20 to 20
- start: float32 [512, 64], replicated, may hold values from -6 to 6
Outputs:
- core: float32 [4, 4, 64, 32768], P('ta', None, 'gx', 'yz')
The draws below stay inside these ranges and needn't reach their ends.
All inputs are finite; a program needn't handle non-finite values.
Results may differ from the reference program's by a relative error of at most 0.0003.
Values sent between devices are 32-bit elements; how exact they have to be, the bound alone decides.
No kernel may reach another device: no remote copies, remote signals or barrier semaphores. Data moves between devices by JAX's collectives and lax.ppermute only.
A program may use at most 64 MiB of HBM per device.

```python
import math
import jax
import jax.numpy as jnp
from jax import lax

NX = 512
RANK = 64
SPECIES = 4
ITERS = 2
PLANES = 32768
TIMES = 4


def draw_field(key, part):
    key = jax.random.fold_in(key, 1)
    k_rows, k_common, k_base, k_shared = jax.random.split(key, 4)
    row_scale = jnp.exp(jax.random.uniform(k_rows, (NX,), jnp.float32, 0.0, math.log(3.0)))
    common = 0.3 * jax.random.truncated_normal(k_common, -4.0, 4.0, (NX,), jnp.float32)
    base = jax.random.truncated_normal(k_base, -4.0, 4.0, (TIMES, SPECIES, NX, PLANES), jnp.float32)
    shared = jax.random.truncated_normal(k_shared, -4.0, 4.0, (TIMES, SPECIES, 1, PLANES), jnp.float32)
    return row_scale[:, None] * base + common[:, None] * shared


def gaussian(stream_key, shape, width, limit, kind=jnp.bfloat16):
    array = jax.random.normal(stream_key, shape, jnp.float32) * width
    return jnp.minimum(jnp.maximum(array, -limit), limit).astype(kind)


def setup_inputs(seed: int = 0) -> dict:
    key_list = jax.random.split(jax.random.key(seed), 3)
    field = draw_field(jax.random.fold_in(key_list[2], 71), 0)
    start = gaussian(key_list[1], (NX, RANK), 1.0, 6.0, jnp.float32)
    return {"field": field, "start": start}


def orthonormal(image):
    small = jnp.dot(image.T, image, precision=lax.Precision.HIGHEST)
    lower = jnp.linalg.cholesky(small)
    return lax.linalg.triangular_solve(lower, image, left_side=False, lower=True, transpose_a=True)

def reference(field, start):
    gram = jnp.zeros((NX, NX), jnp.float32)
    for moment in range(field.shape[0]):
        for specie in range(field.shape[1]):
            block = field[moment, specie]
            gram = gram + jnp.dot(block, block.T, precision=lax.Precision.HIGHEST)
    count = field.shape[0] * field.shape[1] * field.shape[3]
    gram = gram / jnp.float32(count)
    basis = start
    for step in range(ITERS):
        basis = orthonormal(jnp.dot(gram, basis, precision=lax.Precision.HIGHEST))
    return jnp.einsum('ir,tsip->tsrp', basis, field, precision=lax.Precision.HIGHEST)
```

```python
import functools

import jax
import jax.numpy as jnp
from jax import lax
from jax.experimental import pallas as pl
from jax.experimental.pallas import tpu as pltpu
from jax.sharding import Mesh, PartitionSpec as P

ITERS = 2
LANES = 128
VMEM = pl.BlockSpec(memory_space=pltpu.VMEM)


def split(x):
    high = x.astype(jnp.bfloat16)
    return high, (x - high.astype(jnp.float32)).astype(jnp.bfloat16)


def pack_kernel(field_ref, out_ref):
    out_ref[0] = field_ref[...]


def pack(field, groups):
    moments, rows, _ = field.shape
    return pl.pallas_call(
        pack_kernel,
        grid=(groups,),
        in_specs=[pl.BlockSpec((moments, rows, LANES), lambda g: (0, 0, g))],
        out_specs=pl.BlockSpec((1, moments, rows, LANES), lambda g: (g, 0, 0, 0)),
        out_shape=jax.ShapeDtypeStruct((groups, moments, rows, LANES), jnp.float32),
    )(field)


def columns(wide_ref):
    groups, moments, rows, _ = wide_ref.shape
    return jnp.concatenate(
        [wide_ref[:, m].reshape(groups * rows, LANES) for m in range(moments)], axis=1
    )


def blocks(order):
    count = order // LANES
    return [(i, j) for i in range(count) for j in range(i, count)]


def gram_kernel(scale, wide_ref, out_ref):
    high, low = split(columns(wide_ref))
    order = high.shape[0]
    half = order // 2
    dims = (((1,), (1,)), ((), ()))
    dot = functools.partial(lax.dot_general, dimension_numbers=dims, preferred_element_type=jnp.float32)
    parts = {}
    for i in range(2):
        for j in range(i, 2):
            a, b = slice(i * half, (i + 1) * half), slice(j * half, (j + 1) * half)
            parts[i, j] = dot(high[a], high[b]) + (dot(high[a], low[b]) + dot(low[a], high[b]))
    per = half // LANES
    for place, (i, j) in enumerate(blocks(order)):
        part = parts[i // per, j // per]
        r, c = (i % per) * LANES, (j % per) * LANES
        out_ref[place * LANES : (place + 1) * LANES, :] = part[r : r + LANES, c : c + LANES] * scale


def inverse_factor(small):
    n = small.shape[0]
    row = lax.broadcasted_iota(jnp.int32, (n, n), 0)
    lane = lax.broadcasted_iota(jnp.int32, (n, n), 1)
    eye = (row == lane).astype(jnp.float32)
    work = jnp.concatenate([small, eye], axis=1)
    tiles = [work[8 * k : 8 * k + 8] for k in range(n // 8)]
    sub = lax.broadcasted_iota(jnp.int32, (8, 2 * n), 0)
    for j in range(n):
        k0, s = divmod(j, 8)
        pivot_row = jnp.broadcast_to(tiles[k0][s : s + 1, :], (8, 2 * n))
        inverse = 1.0 / jnp.broadcast_to(tiles[k0][s : s + 1, j : j + 1], (8, 2 * n))
        scaled = pivot_row * inverse
        for k in range(k0, n // 8):
            factor = jnp.broadcast_to(tiles[k][:, j : j + 1], (8, 2 * n))
            if k == k0:
                factor = jnp.where(sub > s, factor, 0.0)
            tiles[k] = tiles[k] - factor * scaled
    work = jnp.concatenate(tiles, axis=0)
    pivots = jnp.sum(jnp.where(row == lane, work[:, :n], 0.0), axis=1, keepdims=True)
    return work[:, n:] * lax.rsqrt(pivots)


def core_kernel(gram_ref, start_ref, wide_ref, out_ref, full_ref):
    order = full_ref.shape[0]
    for place, (i, j) in enumerate(blocks(order)):
        block = gram_ref[place * LANES : (place + 1) * LANES, :]
        full_ref[i * LANES : (i + 1) * LANES, j * LANES : (j + 1) * LANES] = block
        if i != j:
            full_ref[j * LANES : (j + 1) * LANES, i * LANES : (i + 1) * LANES] = block.T
    dot = functools.partial(jnp.dot, precision=lax.Precision.HIGHEST, preferred_element_type=jnp.float32)
    basis = start_ref[...]
    for step in range(ITERS):
        image = dot(basis, full_ref[...])
        small = lax.dot_general(
            image,
            image,
            (((1,), (1,)), ((), ())),
            precision=lax.Precision.HIGHEST,
            preferred_element_type=jnp.float32,
        )
        basis = dot(inverse_factor(small), image)
    high, low = split(basis)
    groups, moments, rows, _ = wide_ref.shape
    share = out_ref.shape[2]
    for m in range(moments):
        part_high, part_low = split(wide_ref[:, m].reshape(groups * rows, LANES))
        two = functools.partial(jnp.dot, preferred_element_type=jnp.float32)
        core = two(high, part_high) + (two(high, part_low) + two(low, part_high))
        out_ref[:, m] = core.reshape(groups, share, LANES)


def exchange(x, axes):
    return lax.all_to_all(x, axes, 0, 0, tiled=True)


def shards(count, group_axes, plane_axes, line_axes, field, start):
    groups = lax.axis_size(group_axes)
    flat = lax.axis_size(plane_axes)
    line = lax.axis_size(line_axes)
    times, species, rows, planes = field.shape
    moments = times * species
    order, rank = start.shape
    params = pltpu.CompilerParams(vmem_limit_bytes=40 * 1024 * 1024)

    packed = pack(field.reshape(moments, rows, planes), groups)
    wide = exchange(packed, group_axes)

    depth = len(blocks(order)) * LANES
    partial_gram = pl.pallas_call(
        functools.partial(gram_kernel, 1.0 / count),
        in_specs=[VMEM],
        out_specs=VMEM,
        out_shape=jax.ShapeDtypeStruct((depth, LANES), jnp.float32),
        compiler_params=params,
    )(wide)

    share = depth // flat
    pieces = exchange(partial_gram.reshape(flat, share, LANES), plane_axes)
    mine = jnp.sum(pieces, axis=0)
    mine = jnp.sum(exchange(jnp.broadcast_to(mine, (line, share, LANES)), line_axes), axis=0)
    gram = exchange(jnp.broadcast_to(mine, (flat, share, LANES)), plane_axes).reshape(depth, LANES)

    plane_core = pl.pallas_call(
        core_kernel,
        in_specs=[VMEM] * 3,
        out_specs=VMEM,
        out_shape=jax.ShapeDtypeStruct((groups, moments, rank // groups, LANES), jnp.float32),
        scratch_shapes=[pltpu.VMEM((order, order), jnp.float32)],
        compiler_params=params,
    )(gram, start.T, wide)
    core = exchange(plane_core, group_axes)
    core = jnp.transpose(core, (1, 2, 0, 3))
    return core.reshape(times, species, rank // groups, planes)


def solution(mesh):
    fine = Mesh(
        mesh.devices.reshape(4, 2, 8, 4, 2), ("y", "core", "z_lo", "x", "z_hi")
    )
    placed = P("z_hi", None, ("y", "core"), ("z_lo", "x"))

    def program(field, start):
        count = field.shape[0] * field.shape[1] * field.shape[3]
        body = functools.partial(
            shards, count, ("y", "core"), ("y", "core", "x"), ("z_lo", "z_hi")
        )
        return jax.shard_map(
            body, mesh=fine, in_specs=(placed, P()), out_specs=placed, check_vma=False
        )(field, start)

    return program
```

```python
import functools

import jax
import jax.numpy as jnp
from jax import lax
from jax.experimental import pallas as pl
from jax.experimental.pallas import tpu as pltpu
from jax.sharding import Mesh, PartitionSpec as P

ITERS = 2
LANES = 128
VMEM = pl.BlockSpec(memory_space=pltpu.VMEM)


def split(x):
    high = x.astype(jnp.bfloat16)
    return high, (x - high.astype(jnp.float32)).astype(jnp.bfloat16)


def columns(wide_ref):
    groups, moments, rows, _ = wide_ref.shape
    return jnp.concatenate(
        [wide_ref[:, m].reshape(groups * rows, LANES) for m in range(moments)], axis=1
    )


def blocks(order):
    count = order // LANES
    return [(i, j) for i in range(count) for j in range(i, count)]


def gram_kernel(scale, wide_ref, out_ref):
    high, low = split(columns(wide_ref))
    order = high.shape[0]
    half = order // 2
    dims = (((1,), (1,)), ((), ()))
    dot = functools.partial(lax.dot_general, dimension_numbers=dims, preferred_element_type=jnp.float32)
    parts = {}
    for i in range(2):
        for j in range(i, 2):
            a, b = slice(i * half, (i + 1) * half), slice(j * half, (j + 1) * half)
            parts[i, j] = dot(high[a], high[b]) + (dot(high[a], low[b]) + dot(low[a], high[b]))
    per = half // LANES
    for place, (i, j) in enumerate(blocks(order)):
        part = parts[i // per, j // per]
        r, c = (i % per) * LANES, (j % per) * LANES
        out_ref[place * LANES : (place + 1) * LANES, :] = part[r : r + LANES, c : c + LANES] * scale


def inverse_factor(work):
    n = work.shape[0]
    shape = (8, 2 * n)
    panels = n // 8
    tiles = [work[8 * k : 8 * k + 8] for k in range(panels)]
    sub = lax.broadcasted_iota(jnp.int32, shape, 0)
    done = []
    for p in range(panels):
        at = n + 8 * p
        columns_of = [jnp.broadcast_to(tiles[p][:, at + j : at + j + 1], shape) for j in range(8)]
        rows = [jnp.broadcast_to(tiles[p][i : i + 1], shape) for i in range(8)]
        pivot = {
            (i, j): jnp.broadcast_to(columns_of[j][i : i + 1], shape) for j in range(8) for i in range(j, 8)
        }
        factor, inverse = {}, []
        for i in range(8):
            inverse.append(1.0 / pivot[i, i])
            for j in range(i + 1, 8):
                factor[j, i] = pivot[j, i] * inverse[i]
            for j in range(i + 1, 8):
                for m in range(i + 1, j + 1):
                    pivot[j, m] = pivot[j, m] - factor[j, i] * pivot[m, i]
                rows[j] = rows[j] - factor[j, i] * rows[i]
        final = rows[0] * lax.rsqrt(pivot[0, 0])
        for i in range(1, 8):
            final = jnp.where(sub == i, rows[i] * lax.rsqrt(pivot[i, i]), final)
        done.append(final)
        solved = [None] * 8
        for i in range(7, -1, -1):
            value = rows[i] * inverse[i]
            for k in range(i + 1, 8):
                value = value - factor[k, i] * solved[k]
            solved[i] = value
        for t in range(p + 1, panels):
            terms = [
                jnp.broadcast_to(tiles[t][:, at + j : at + j + 1], shape) * solved[j] for j in range(8)
            ]
            while len(terms) > 1:
                terms = [x + y for x, y in zip(terms[::2], terms[1::2])]
            tiles[t] = tiles[t] - terms[0]
    return jnp.concatenate(done, axis=0)[:, :n]


def core_kernel(gram_ref, start_ref, wide_ref, out_ref, full_ref):
    order = full_ref.shape[0]
    for place, (i, j) in enumerate(blocks(order)):
        block = gram_ref[place * LANES : (place + 1) * LANES, :]
        full_ref[i * LANES : (i + 1) * LANES, j * LANES : (j + 1) * LANES] = block
        if i != j:
            full_ref[j * LANES : (j + 1) * LANES, i * LANES : (i + 1) * LANES] = block.T
    dot = functools.partial(jnp.dot, precision=lax.Precision.HIGHEST, preferred_element_type=jnp.float32)
    basis = start_ref[...]
    rank = basis.shape[0]
    shape = (rank, 2 * rank)
    row, lane = (lax.broadcasted_iota(jnp.int32, shape, axis) for axis in (0, 1))
    eye = (row == lane).astype(jnp.float32)
    for step in range(ITERS):
        image = dot(basis, full_ref[...])
        small = lax.dot_general(
            image,
            jnp.concatenate([jnp.zeros_like(image), image], axis=0),
            (((1,), (1,)), ((), ())),
            precision=lax.Precision.HIGHEST,
            preferred_element_type=jnp.float32,
        )
        basis = dot(inverse_factor(small + eye), image)
    high, low = split(basis)
    groups, moments, rows, _ = wide_ref.shape
    share = out_ref.shape[2]
    for m in range(moments):
        part_high, part_low = split(wide_ref[:, m].reshape(groups * rows, LANES))
        two = functools.partial(jnp.dot, preferred_element_type=jnp.float32)
        core = two(high, part_high) + (two(high, part_low) + two(low, part_high))
        out_ref[:, m] = core.reshape(groups, share, LANES)


def exchange(x, axes):
    return lax.all_to_all(x, axes, 0, 0, tiled=True)


def shards(count, group_axes, plane_axes, line_axes, field, start):
    groups = lax.axis_size(group_axes)
    flat = lax.axis_size(plane_axes)
    times, species, rows, planes = field.shape
    moments = times * species
    order, rank = start.shape
    params = pltpu.CompilerParams(vmem_limit_bytes=40 * 1024 * 1024)

    tiles = field.reshape(moments, rows // 8, 8, groups, LANES)
    packed = jnp.transpose(tiles, (3, 0, 1, 2, 4)).reshape(groups, moments, rows, LANES)
    wide = exchange(packed, group_axes)

    depth = len(blocks(order)) * LANES
    partial_gram = pl.pallas_call(
        functools.partial(gram_kernel, 1.0 / count),
        in_specs=[VMEM],
        out_specs=VMEM,
        out_shape=jax.ShapeDtypeStruct((depth, LANES), jnp.float32),
        compiler_params=params,
    )(wide)

    share = depth // flat
    pieces = exchange(partial_gram.reshape(flat, share, LANES), plane_axes)
    mine = jnp.sum(pieces, axis=0)
    for axes in line_axes:
        spread = jnp.broadcast_to(mine, (lax.axis_size(axes), share, LANES))
        mine = jnp.sum(exchange(spread, axes), axis=0)
    gram = exchange(jnp.broadcast_to(mine, (flat, share, LANES)), plane_axes).reshape(depth, LANES)

    plane_core = pl.pallas_call(
        core_kernel,
        in_specs=[VMEM] * 3,
        out_specs=VMEM,
        out_shape=jax.ShapeDtypeStruct((groups, moments, rank // groups, LANES), jnp.float32),
        scratch_shapes=[pltpu.VMEM((order, order), jnp.float32)],
        compiler_params=params,
    )(gram, start.T, wide)
    core = exchange(plane_core, group_axes)
    core = jnp.transpose(core, (1, 2, 0, 3))
    return core.reshape(times, species, rank // groups, planes)


def solution(mesh):
    fine = Mesh(
        mesh.devices.reshape(4, 2, 2, 4, 4, 2), ("y", "core", "z_mid", "z_near", "x", "z_hi")
    )
    placed = P("z_hi", None, ("y", "core"), ("z_mid", "z_near", "x"))

    def program(field, start):
        count = field.shape[0] * field.shape[1] * field.shape[3]
        body = functools.partial(
            shards, count, ("y", "core"), ("y", "core", "x"), ("z_near", ("z_mid", "z_hi"))
        )
        return jax.shard_map(
            body, mesh=fine, in_specs=(placed, P()), out_specs=placed, check_vma=False
        )(field, start)

    return program
```

```python
import functools

import jax
import jax.numpy as jnp
from jax import lax
from jax.experimental import pallas as pl
from jax.experimental.pallas import tpu as pltpu
from jax.sharding import Mesh, PartitionSpec as P

ITERS = 2
LANES = 128
SLAB = 4
VMEM = pl.BlockSpec(memory_space=pltpu.VMEM)


def split(x):
    high = x.astype(jnp.bfloat16)
    return high, (x - high.astype(jnp.float32)).astype(jnp.bfloat16)


def columns(wide_ref):
    groups, moments, rows, _ = wide_ref.shape
    return jnp.concatenate(
        [wide_ref[:, m].reshape(groups * rows, LANES) for m in range(moments)], axis=1
    )


def blocks(order):
    count = order // LANES
    return [(i, j) for i in range(count) for j in range(i, count)]


def gram_kernel(scale, wide_ref, out_ref):
    high, low = split(columns(wide_ref))
    order = high.shape[0]
    half = order // 2
    dims = (((1,), (1,)), ((), ()))
    dot = functools.partial(lax.dot_general, dimension_numbers=dims, preferred_element_type=jnp.float32)
    parts = {}
    for i in range(2):
        for j in range(i, 2):
            a, b = slice(i * half, (i + 1) * half), slice(j * half, (j + 1) * half)
            parts[i, j] = dot(high[a], high[b]) + (dot(high[a], low[b]) + dot(low[a], high[b]))
    per = half // LANES
    for place, (i, j) in enumerate(blocks(order)):
        part = parts[i // per, j // per]
        r, c = (i % per) * LANES, (j % per) * LANES
        out_ref[place * LANES : (place + 1) * LANES, :] = part[r : r + LANES, c : c + LANES] * scale


def inverse_factor(work):
    n = work.shape[0]
    shape = (8, 2 * n)
    panels = n // 8
    tiles = [work[8 * k : 8 * k + 8] for k in range(panels)]
    sub = lax.broadcasted_iota(jnp.int32, shape, 0)
    done = []
    for p in range(panels):
        at = n + 8 * p
        columns_of = [jnp.broadcast_to(tiles[p][:, at + j : at + j + 1], shape) for j in range(8)]
        rows = [jnp.broadcast_to(tiles[p][i : i + 1], shape) for i in range(8)]
        pivot = {
            (i, j): jnp.broadcast_to(columns_of[j][i : i + 1], shape) for j in range(8) for i in range(j, 8)
        }
        factor, inverse = {}, []
        for i in range(8):
            inverse.append(1.0 / pivot[i, i])
            for j in range(i + 1, 8):
                factor[j, i] = pivot[j, i] * inverse[i]
            for j in range(i + 1, 8):
                for m in range(i + 1, j + 1):
                    pivot[j, m] = pivot[j, m] - factor[j, i] * pivot[m, i]
                rows[j] = rows[j] - factor[j, i] * rows[i]
        final = rows[0] * lax.rsqrt(pivot[0, 0])
        for i in range(1, 8):
            final = jnp.where(sub == i, rows[i] * lax.rsqrt(pivot[i, i]), final)
        done.append(final)
        solved = [None] * 8
        for i in range(7, -1, -1):
            value = rows[i] * inverse[i]
            for k in range(i + 1, 8):
                value = value - factor[k, i] * solved[k]
            solved[i] = value
        for t in range(p + 1, panels):
            terms = [
                jnp.broadcast_to(tiles[t][:, at + j : at + j + 1], shape) * solved[j] for j in range(8)
            ]
            while len(terms) > 1:
                terms = [x + y for x, y in zip(terms[::2], terms[1::2])]
            tiles[t] = tiles[t] - terms[0]
    return jnp.concatenate(done, axis=0)[:, :n]


def core_kernel(gram_ref, start_ref, wide_ref, out_ref, full_ref):
    order = full_ref.shape[0]
    for place, (i, j) in enumerate(blocks(order)):
        block = gram_ref[place * LANES : (place + 1) * LANES, :]
        full_ref[i * LANES : (i + 1) * LANES, j * LANES : (j + 1) * LANES] = block
        if i != j:
            full_ref[j * LANES : (j + 1) * LANES, i * LANES : (i + 1) * LANES] = block.T
    dot = functools.partial(jnp.dot, precision=lax.Precision.HIGHEST, preferred_element_type=jnp.float32)
    basis = start_ref[...]
    rank = basis.shape[0]
    shape = (rank, 2 * rank)
    row, lane = (lax.broadcasted_iota(jnp.int32, shape, axis) for axis in (0, 1))
    eye = (row == lane).astype(jnp.float32)
    for step in range(ITERS):
        image = dot(basis, full_ref[...])
        small = lax.dot_general(
            image,
            jnp.concatenate([jnp.zeros_like(image), image], axis=0),
            (((1,), (1,)), ((), ())),
            precision=lax.Precision.HIGHEST,
            preferred_element_type=jnp.float32,
        )
        basis = dot(inverse_factor(small + eye), image)
    high, low = split(basis)
    groups, moments, rows, _ = wide_ref.shape
    share = out_ref.shape[2]
    for m in range(moments):
        part_high, part_low = split(wide_ref[:, m].reshape(groups * rows, LANES))
        two = functools.partial(jnp.dot, preferred_element_type=jnp.float32)
        core = two(high, part_high) + (two(high, part_low) + two(low, part_high))
        out_ref[:, m] = core.reshape(groups, share, LANES)


def exchange(x, axes):
    return lax.all_to_all(x, axes, 0, 0, tiled=True)


def added(pieces, count):
    return jnp.sum(pieces.reshape(count, pieces.shape[0] // count, *pieces.shape[1:]), axis=0)


def spread(block, count):
    copies = jnp.broadcast_to(block, (count, *block.shape))
    return copies.reshape(count * block.shape[0], *block.shape[1:])


def shards(count, group_axes, plane_axes, line_axes, field, start):
    groups = lax.axis_size(group_axes)
    flat = lax.axis_size(plane_axes)
    line = lax.axis_size(line_axes)
    times, species, rows, planes = field.shape
    moments = times * species
    order, rank = start.shape
    params = pltpu.CompilerParams(vmem_limit_bytes=40 * 1024 * 1024)

    tiles = field.reshape(moments, rows // 8, 8, groups, LANES)
    packed = jnp.transpose(tiles, (3, 0, 1, 2, 4)).reshape(groups, moments, rows, LANES)
    wide = exchange(packed, group_axes)

    depth = len(blocks(order)) * LANES
    partial_gram = pl.pallas_call(
        functools.partial(gram_kernel, 1.0 / count),
        in_specs=[VMEM],
        out_specs=VMEM,
        out_shape=jax.ShapeDtypeStruct((depth, LANES), jnp.float32),
        compiler_params=params,
    )(wide)

    share = depth // flat // SLAB
    pieces = exchange(partial_gram.reshape(flat * share, SLAB, LANES), plane_axes)
    mine = added(pieces, flat)
    mine = added(exchange(spread(mine, line), line_axes), line)
    gram = exchange(spread(mine, flat), plane_axes).reshape(depth, LANES)

    plane_core = pl.pallas_call(
        core_kernel,
        in_specs=[VMEM] * 3,
        out_specs=VMEM,
        out_shape=jax.ShapeDtypeStruct((groups, moments, rank // groups, LANES), jnp.float32),
        scratch_shapes=[pltpu.VMEM((order, order), jnp.float32)],
        compiler_params=params,
    )(gram, start.T, wide)
    core = exchange(plane_core, group_axes)
    core = jnp.transpose(core, (1, 2, 0, 3))
    return core.reshape(times, species, rank // groups, planes)


def solution(mesh):
    fine = Mesh(
        mesh.devices.reshape(4, 2, 4, 2, 4, 2), ("y", "core", "z_mid", "z_pair", "x", "z_hi")
    )
    placed = P("z_hi", None, ("y", "core"), ("z_mid", "z_pair", "x"))

    def program(field, start):
        count = field.shape[0] * field.shape[1] * field.shape[3]
        body = functools.partial(
            shards, count, ("y", "core"), ("y", "core", "z_pair", "x"), ("z_mid", "z_hi")
        )
        return jax.shard_map(
            body, mesh=fine, in_specs=(placed, P()), out_specs=placed, check_vma=False
        )(field, start)

    return program
```

```python
import functools

import jax
import jax.numpy as jnp
from jax import lax
from jax.experimental import pallas as pl
from jax.experimental.pallas import tpu as pltpu
from jax.sharding import Mesh, PartitionSpec as P

ITERS = 2
LANES = 128
SLAB = 4
VMEM = pl.BlockSpec(memory_space=pltpu.VMEM)


def split(x):
    high = x.astype(jnp.bfloat16)
    return high, (x - high.astype(jnp.float32)).astype(jnp.bfloat16)


def blocks(order):
    count = order // LANES
    return [(i, j) for i in range(count) for j in range(i, count)]


def gram_kernel(scale, wide_ref, out_ref):
    high, low = split(wide_ref[...])
    order = high.shape[0]
    half = order // 2
    dims = (((1,), (1,)), ((), ()))
    dot = functools.partial(lax.dot_general, dimension_numbers=dims, preferred_element_type=jnp.float32)
    parts = {}
    for i in range(2):
        for j in range(i, 2):
            a, b = slice(i * half, (i + 1) * half), slice(j * half, (j + 1) * half)
            parts[i, j] = dot(high[a], high[b]) + (dot(high[a], low[b]) + dot(low[a], high[b]))
    per = half // LANES
    for place, (i, j) in enumerate(blocks(order)):
        part = parts[i // per, j // per]
        r, c = (i % per) * LANES, (j % per) * LANES
        out_ref[place * LANES : (place + 1) * LANES, :] = part[r : r + LANES, c : c + LANES] * scale


def inverse_factor(work):
    n = work.shape[0]
    shape = (8, 2 * n)
    panels = n // 8
    tiles = [work[8 * k : 8 * k + 8] for k in range(panels)]
    sub = lax.broadcasted_iota(jnp.int32, shape, 0)
    done = []
    for p in range(panels):
        at = n + 8 * p
        columns_of = [jnp.broadcast_to(tiles[p][:, at + j : at + j + 1], shape) for j in range(8)]
        rows = [jnp.broadcast_to(tiles[p][i : i + 1], shape) for i in range(8)]
        pivot = {
            (i, j): jnp.broadcast_to(columns_of[j][i : i + 1], shape) for j in range(8) for i in range(j, 8)
        }
        factor, inverse = {}, []
        for i in range(8):
            inverse.append(1.0 / pivot[i, i])
            for j in range(i + 1, 8):
                factor[j, i] = pivot[j, i] * inverse[i]
            for j in range(i + 1, 8):
                for m in range(i + 1, j + 1):
                    pivot[j, m] = pivot[j, m] - factor[j, i] * pivot[m, i]
                rows[j] = rows[j] - factor[j, i] * rows[i]
        final = rows[0] * lax.rsqrt(pivot[0, 0])
        for i in range(1, 8):
            final = jnp.where(sub == i, rows[i] * lax.rsqrt(pivot[i, i]), final)
        done.append(final)
        solved = [None] * 8
        for i in range(7, -1, -1):
            value = rows[i] * inverse[i]
            for k in range(i + 1, 8):
                value = value - factor[k, i] * solved[k]
            solved[i] = value
        for t in range(p + 1, panels):
            terms = [
                jnp.broadcast_to(tiles[t][:, at + j : at + j + 1], shape) * solved[j] for j in range(8)
            ]
            while len(terms) > 1:
                terms = [x + y for x, y in zip(terms[::2], terms[1::2])]
            tiles[t] = tiles[t] - terms[0]
    return jnp.concatenate(done, axis=0)[:, :n]


def core_kernel(gram_ref, start_ref, wide_ref, out_ref, full_ref):
    order = full_ref.shape[0]
    for place, (i, j) in enumerate(blocks(order)):
        block = gram_ref[place * LANES : (place + 1) * LANES, :]
        full_ref[i * LANES : (i + 1) * LANES, j * LANES : (j + 1) * LANES] = block
        if i != j:
            full_ref[j * LANES : (j + 1) * LANES, i * LANES : (i + 1) * LANES] = block.T
    dot = functools.partial(jnp.dot, precision=lax.Precision.HIGHEST, preferred_element_type=jnp.float32)
    basis = start_ref[...]
    rank = basis.shape[0]
    shape = (rank, 2 * rank)
    row, lane = (lax.broadcasted_iota(jnp.int32, shape, axis) for axis in (0, 1))
    eye = (row == lane).astype(jnp.float32)
    for step in range(ITERS):
        image = dot(basis, full_ref[...])
        small = lax.dot_general(
            image,
            jnp.concatenate([jnp.zeros_like(image), image], axis=0),
            (((1,), (1,)), ((), ())),
            precision=lax.Precision.HIGHEST,
            preferred_element_type=jnp.float32,
        )
        basis = dot(inverse_factor(small + eye), image)
    high, low = split(basis)
    part_high, part_low = split(wide_ref[...])
    two = functools.partial(jnp.dot, preferred_element_type=jnp.float32)
    out_ref[...] = two(high, part_high) + (two(high, part_low) + two(low, part_high))


def exchange(x, axes):
    return lax.all_to_all(x, axes, 0, 0, tiled=True)


def added(pieces, count):
    return jnp.sum(pieces.reshape(count, pieces.shape[0] // count, *pieces.shape[1:]), axis=0)


def spread(block, count):
    copies = jnp.broadcast_to(block, (count, *block.shape))
    return copies.reshape(count * block.shape[0], *block.shape[1:])


def shards(count, group_axes, plane_axes, line_axes, field, start):
    groups = lax.axis_size(group_axes)
    flat = lax.axis_size(plane_axes)
    line = lax.axis_size(line_axes)
    times, species, rows, planes = field.shape
    moments = times * species
    order, rank = start.shape
    params = pltpu.CompilerParams(vmem_limit_bytes=40 * 1024 * 1024)

    wide = exchange(field.reshape(moments, rows, planes), group_axes)
    wide = wide.reshape(groups, moments // groups, rows, planes)
    wide = jnp.moveaxis(wide, 1, 2).reshape(order, moments // groups * planes)

    depth = len(blocks(order)) * LANES
    partial_gram = pl.pallas_call(
        functools.partial(gram_kernel, 1.0 / count),
        in_specs=[VMEM],
        out_specs=VMEM,
        out_shape=jax.ShapeDtypeStruct((depth, LANES), jnp.float32),
        compiler_params=params,
    )(wide)

    share = depth // flat // SLAB
    pieces = exchange(partial_gram.reshape(flat * share, SLAB, LANES), plane_axes)
    mine = added(pieces, flat)
    mine = added(exchange(spread(mine, line), line_axes), line)
    gram = exchange(spread(mine, flat), plane_axes).reshape(depth, LANES)

    plane_core = pl.pallas_call(
        core_kernel,
        in_specs=[VMEM] * 3,
        out_specs=VMEM,
        out_shape=jax.ShapeDtypeStruct((rank, wide.shape[1]), jnp.float32),
        scratch_shapes=[pltpu.VMEM((order, order), jnp.float32)],
        compiler_params=params,
    )(gram, start.T, wide)
    plane_core = plane_core.reshape(rank, moments // groups, planes)
    plane_core = plane_core.reshape(groups, rank // groups, moments // groups, planes)
    core = exchange(jnp.moveaxis(plane_core, 2, 1).reshape(moments, rank // groups, planes), group_axes)
    return core.reshape(times, species, rank // groups, planes)


def solution(mesh):
    fine = Mesh(
        mesh.devices.reshape(4, 2, 4, 2, 4, 2), ("y", "core", "z_mid", "z_pair", "x", "z_hi")
    )
    placed = P("z_hi", None, ("y", "core"), ("z_mid", "z_pair", "x"))

    def program(field, start):
        count = field.shape[0] * field.shape[1] * field.shape[3]
        body = functools.partial(
            shards, count, ("y", "core"), ("y", "core", "z_pair", "x"), ("z_mid", "z_hi")
        )
        return jax.shard_map(
            body, mesh=fine, in_specs=(placed, P()), out_specs=placed, check_vma=False
        )(field, start)

    return program
```

```python
import functools

import jax
import jax.numpy as jnp
from jax import lax
from jax.experimental import pallas as pl
from jax.experimental.pallas import tpu as pltpu
from jax.sharding import Mesh, PartitionSpec as P

ITERS = 2
LANES = 128
SLAB = 4
VMEM = pl.BlockSpec(memory_space=pltpu.VMEM)


def split(x):
    high = x.astype(jnp.bfloat16)
    return high, (x - high.astype(jnp.float32)).astype(jnp.bfloat16)


def blocks(order):
    count = order // LANES
    return [(i, j) for i in range(count) for j in range(i, count)]


def gram_kernel(scale, wide_ref, out_ref):
    high, low = split(wide_ref[...])
    order = high.shape[0]
    half = order // 2
    dims = (((1,), (1,)), ((), ()))
    dot = functools.partial(lax.dot_general, dimension_numbers=dims, preferred_element_type=jnp.float32)
    parts = {}
    for i in range(2):
        for j in range(i, 2):
            a, b = slice(i * half, (i + 1) * half), slice(j * half, (j + 1) * half)
            parts[i, j] = dot(high[a], high[b]) + (dot(high[a], low[b]) + dot(low[a], high[b]))
    per = half // LANES
    for place, (i, j) in enumerate(blocks(order)):
        part = parts[i // per, j // per]
        r, c = (i % per) * LANES, (j % per) * LANES
        out_ref[place * LANES : (place + 1) * LANES, :] = part[r : r + LANES, c : c + LANES] * scale


def inverse_factor(work):
    n = work.shape[0]
    shape = (8, 2 * n)
    panels = n // 8
    tiles = [work[8 * k : 8 * k + 8] for k in range(panels)]
    sub = lax.broadcasted_iota(jnp.int32, shape, 0)
    done = []
    for p in range(panels):
        at = n + 8 * p
        columns_of = [jnp.broadcast_to(tiles[p][:, at + j : at + j + 1], shape) for j in range(8)]
        rows = [jnp.broadcast_to(tiles[p][i : i + 1], shape) for i in range(8)]
        pivot = {
            (i, j): jnp.broadcast_to(columns_of[j][i : i + 1], shape) for j in range(8) for i in range(j, 8)
        }
        factor, inverse = {}, []
        for i in range(8):
            inverse.append(1.0 / pivot[i, i])
            for j in range(i + 1, 8):
                factor[j, i] = pivot[j, i] * inverse[i]
            for j in range(i + 1, 8):
                for m in range(i + 1, j + 1):
                    pivot[j, m] = pivot[j, m] - factor[j, i] * pivot[m, i]
                rows[j] = rows[j] - factor[j, i] * rows[i]
        final = rows[0] * lax.rsqrt(pivot[0, 0])
        for i in range(1, 8):
            final = jnp.where(sub == i, rows[i] * lax.rsqrt(pivot[i, i]), final)
        done.append(final)
        solved = [None] * 8
        for i in range(7, -1, -1):
            value = rows[i] * inverse[i]
            for k in range(i + 1, 8):
                value = value - factor[k, i] * solved[k]
            solved[i] = value
        for t in range(p + 1, panels):
            terms = [
                jnp.broadcast_to(tiles[t][:, at + j : at + j + 1], shape) * solved[j] for j in range(8)
            ]
            while len(terms) > 1:
                terms = [x + y for x, y in zip(terms[::2], terms[1::2])]
            tiles[t] = tiles[t] - terms[0]
    return jnp.concatenate(done, axis=0)[:, :n]


def core_kernel(gram_ref, start_ref, wide_ref, out_ref, full_ref):
    order = full_ref.shape[0]
    for place, (i, j) in enumerate(blocks(order)):
        block = gram_ref[place * LANES : (place + 1) * LANES, :]
        full_ref[i * LANES : (i + 1) * LANES, j * LANES : (j + 1) * LANES] = block
        if i != j:
            full_ref[j * LANES : (j + 1) * LANES, i * LANES : (i + 1) * LANES] = block.T
    dot = functools.partial(jnp.dot, precision=lax.Precision.HIGHEST, preferred_element_type=jnp.float32)
    basis = start_ref[...]
    rank = basis.shape[0]
    shape = (rank, 2 * rank)
    row, lane = (lax.broadcasted_iota(jnp.int32, shape, axis) for axis in (0, 1))
    eye = (row == lane).astype(jnp.float32)
    for step in range(ITERS):
        image = dot(basis, full_ref[...])
        small = lax.dot_general(
            image,
            jnp.concatenate([jnp.zeros_like(image), image], axis=0),
            (((1,), (1,)), ((), ())),
            precision=lax.Precision.HIGHEST,
            preferred_element_type=jnp.float32,
        )
        basis = dot(inverse_factor(small + eye), image)
    high, low = split(basis)
    part_high, part_low = split(wide_ref[...])
    two = functools.partial(jnp.dot, preferred_element_type=jnp.float32)
    out_ref[...] = two(high, part_high) + (two(high, part_low) + two(low, part_high))


def exchange(x, axes):
    return lax.all_to_all(x, axes, 0, 0, tiled=True)


def added(pieces, count):
    return jnp.sum(pieces.reshape(count, pieces.shape[0] // count, *pieces.shape[1:]), axis=0)


def spread(block, count):
    copies = jnp.broadcast_to(block, (count, *block.shape))
    return copies.reshape(count * block.shape[0], *block.shape[1:])


def shards(count, group_axes, core_axes, plane_axes, line_axes, field, start):
    groups = lax.axis_size(group_axes)
    times, species, rows, planes = field.shape
    moments = times * species
    order, rank = start.shape
    params = pltpu.CompilerParams(vmem_limit_bytes=40 * 1024 * 1024)

    wide = exchange(field.reshape(moments, rows, planes), group_axes)
    wide = wide.reshape(groups, moments // groups, rows, planes)
    wide = jnp.moveaxis(wide, 1, 2).reshape(order, moments // groups * planes)

    depth = len(blocks(order)) * LANES
    partial_gram = pl.pallas_call(
        functools.partial(gram_kernel, 1.0 / count),
        in_specs=[VMEM],
        out_specs=VMEM,
        out_shape=jax.ShapeDtypeStruct((depth, LANES), jnp.float32),
        compiler_params=params,
    )(wide)

    gram = partial_gram.reshape(depth // SLAB, SLAB, LANES)
    for axes in (core_axes, plane_axes):
        gram = added(exchange(gram, axes), lax.axis_size(axes))
    line = lax.axis_size(line_axes)
    gram = added(exchange(spread(gram, line), line_axes), line)
    for axes in (plane_axes, core_axes):
        gram = exchange(spread(gram, lax.axis_size(axes)), axes)
    gram = gram.reshape(depth, LANES)

    plane_core = pl.pallas_call(
        core_kernel,
        in_specs=[VMEM] * 3,
        out_specs=VMEM,
        out_shape=jax.ShapeDtypeStruct((rank, wide.shape[1]), jnp.float32),
        scratch_shapes=[pltpu.VMEM((order, order), jnp.float32)],
        compiler_params=params,
    )(gram, start.T, wide)
    plane_core = plane_core.reshape(rank, moments // groups, planes)
    plane_core = plane_core.reshape(groups, rank // groups, moments // groups, planes)
    core = exchange(jnp.moveaxis(plane_core, 2, 1).reshape(moments, rank // groups, planes), group_axes)
    return core.reshape(times, species, rank // groups, planes)


def solution(mesh):
    fine = Mesh(
        mesh.devices.reshape(4, 2, 4, 2, 4, 2), ("y", "core", "z_mid", "z_pair", "x", "z_hi")
    )
    placed = P("z_hi", None, ("y", "core"), ("z_mid", "z_pair", "x"))

    def program(field, start):
        count = field.shape[0] * field.shape[1] * field.shape[3]
        body = functools.partial(
            shards, count, ("y", "core"), "core", ("y", "z_pair", "x"), ("z_mid", "z_hi")
        )
        return jax.shard_map(
            body, mesh=fine, in_specs=(placed, P()), out_specs=placed, check_vma=False
        )(field, start)

    return program
```

```python
import functools

import jax
import jax.numpy as jnp
from jax import lax
from jax.experimental import pallas as pl
from jax.experimental.pallas import tpu as pltpu
from jax.sharding import Mesh, PartitionSpec as P

ITERS = 2
LANES = 128
SLAB = 4
VMEM = pl.BlockSpec(memory_space=pltpu.VMEM)


def split(x):
    high = x.astype(jnp.bfloat16)
    return high, (x - high.astype(jnp.float32)).astype(jnp.bfloat16)


def blocks(order):
    count = order // LANES
    return [(i, j) for i in range(count) for j in range(i, count)]


def gram_kernel(scale, wide_ref, out_ref):
    high, low = split(wide_ref[...])
    order = high.shape[0]
    half = order // 2
    dims = (((1,), (1,)), ((), ()))
    dot = functools.partial(lax.dot_general, dimension_numbers=dims, preferred_element_type=jnp.float32)
    parts = {}
    for i in range(2):
        for j in range(i, 2):
            a, b = slice(i * half, (i + 1) * half), slice(j * half, (j + 1) * half)
            parts[i, j] = dot(high[a], high[b]) + (dot(high[a], low[b]) + dot(low[a], high[b]))
    per = half // LANES
    for place, (i, j) in enumerate(blocks(order)):
        part = parts[i // per, j // per]
        r, c = (i % per) * LANES, (j % per) * LANES
        out_ref[place * LANES : (place + 1) * LANES, :] = part[r : r + LANES, c : c + LANES] * scale


def inverse_factor(work, column_ref):
    n = work.shape[0]
    shape = (8, 2 * n)
    panels = n // 8
    tiles = [work[8 * k : 8 * k + 8] for k in range(panels)]
    sub = lax.broadcasted_iota(jnp.int32, shape, 0)
    done = []
    for p in range(panels):
        at = n + 8 * p
        rest = range(p + 1, panels)

        def column(tile, j):
            return jnp.broadcast_to(tile[:, at + j : at + j + 1], shape)

        for j in range(8):
            column_ref[p, j] = column(tiles[p], j)
        rows = [jnp.broadcast_to(tiles[p][i : i + 1], shape) for i in range(8)]
        pivot = {
            (i, j): jnp.broadcast_to(column_ref[p, j, i : i + 1, :], shape)
            for j in range(8)
            for i in range(j, 8)
        }
        below = {t: [column(tiles[t], j) for j in range(8)] for t in rest}
        factor, scaled = {}, []
        for i in range(8):
            inverse = 1.0 / pivot[i, i]
            scaled.append(rows[i] * inverse)
            for j in range(i + 1, 8):
                factor[j, i] = pivot[j, i] * inverse
            for j in range(i + 1, 8):
                for m in range(i + 1, j + 1):
                    pivot[j, m] = pivot[j, m] - factor[j, i] * pivot[m, i]
                rows[j] = rows[j] - factor[j, i] * rows[i]
            for t in rest:
                tiles[t] = tiles[t] - below[t][i] * scaled[i]
                for j in range(i + 1, 8):
                    below[t][j] = below[t][j] - factor[j, i] * below[t][i]
        final = rows[0] * lax.rsqrt(pivot[0, 0])
        for i in range(1, 8):
            final = jnp.where(sub == i, rows[i] * lax.rsqrt(pivot[i, i]), final)
        done.append(final)
    return jnp.concatenate(done, axis=0)[:, :n]


def core_kernel(gram_ref, start_ref, wide_ref, out_ref, full_ref, column_ref):
    order = full_ref.shape[0]
    for place, (i, j) in enumerate(blocks(order)):
        block = gram_ref[place * LANES : (place + 1) * LANES, :]
        full_ref[i * LANES : (i + 1) * LANES, j * LANES : (j + 1) * LANES] = block
        if i != j:
            full_ref[j * LANES : (j + 1) * LANES, i * LANES : (i + 1) * LANES] = block.T
    dot = functools.partial(
        lax.dot_general, precision=lax.Precision.HIGHEST, preferred_element_type=jnp.float32
    )
    plain, across = (((1,), (0,)), ((), ())), (((1,), (1,)), ((), ()))
    rank = start_ref.shape[0]
    shape = (rank, 2 * rank)
    row, lane = (lax.broadcasted_iota(jnp.int32, shape, axis) for axis in (0, 1))
    eye = (row == lane).astype(jnp.float32)
    image = dot(start_ref[...], full_ref[...], plain)
    for step in range(ITERS):
        small = dot(image, jnp.concatenate([jnp.zeros_like(image), image], axis=0), across)
        follow = dot(image, full_ref[...] if step + 1 < ITERS else wide_ref[...], plain)
        image = dot(inverse_factor(small + eye, column_ref), follow, plain)
    out_ref[...] = image


def exchange(x, axes):
    return lax.all_to_all(x, axes, 0, 0, tiled=True)


def added(pieces, count):
    return jnp.sum(pieces.reshape(count, pieces.shape[0] // count, *pieces.shape[1:]), axis=0)


def spread(block, count):
    copies = jnp.broadcast_to(block, (count, *block.shape))
    return copies.reshape(count * block.shape[0], *block.shape[1:])


def shards(count, group_axes, core_axes, plane_axes, line_axes, field, start):
    groups = lax.axis_size(group_axes)
    times, species, rows, planes = field.shape
    moments = times * species
    order, rank = start.shape
    params = pltpu.CompilerParams(vmem_limit_bytes=40 * 1024 * 1024)

    wide = exchange(field.reshape(moments, rows, planes), group_axes)
    wide = wide.reshape(groups, moments // groups, rows, planes)
    wide = jnp.moveaxis(wide, 1, 2).reshape(order, moments // groups * planes)

    depth = len(blocks(order)) * LANES
    partial_gram = pl.pallas_call(
        functools.partial(gram_kernel, 1.0 / count),
        in_specs=[VMEM],
        out_specs=VMEM,
        out_shape=jax.ShapeDtypeStruct((depth, LANES), jnp.float32),
        compiler_params=params,
    )(wide)

    gram = partial_gram.reshape(depth // SLAB, SLAB, LANES)
    for axes in (core_axes, plane_axes):
        gram = added(exchange(gram, axes), lax.axis_size(axes))
    line = lax.axis_size(line_axes)
    gram = added(exchange(spread(gram, line), line_axes), line)
    for axes in (plane_axes, core_axes):
        gram = exchange(spread(gram, lax.axis_size(axes)), axes)
    gram = gram.reshape(depth, LANES)

    plane_core = pl.pallas_call(
        core_kernel,
        in_specs=[VMEM] * 3,
        out_specs=VMEM,
        out_shape=jax.ShapeDtypeStruct((rank, wide.shape[1]), jnp.float32),
        scratch_shapes=[
            pltpu.VMEM((order, order), jnp.float32),
            pltpu.VMEM((rank // 8, 8, 8, 2 * rank), jnp.float32),
        ],
        compiler_params=params,
    )(gram, start.T, wide)
    plane_core = plane_core.reshape(rank, moments // groups, planes)
    plane_core = plane_core.reshape(groups, rank // groups, moments // groups, planes)
    core = exchange(jnp.moveaxis(plane_core, 2, 1).reshape(moments, rank // groups, planes), group_axes)
    return core.reshape(times, species, rank // groups, planes)


def solution(mesh):
    fine = Mesh(
        mesh.devices.reshape(4, 2, 4, 2, 4, 2), ("y", "core", "z_mid", "z_pair", "x", "z_hi")
    )
    placed = P("z_hi", None, ("y", "core"), ("z_mid", "z_pair", "x"))

    def program(field, start):
        count = field.shape[0] * field.shape[1] * field.shape[3]
        body = functools.partial(
            shards, count, ("y", "core"), "core", ("y", "z_pair", "x"), ("z_mid", "z_hi")
        )
        return jax.shard_map(
            body, mesh=fine, in_specs=(placed, P()), out_specs=placed, check_vma=False
        )(field, start)

    return program
```

```python
import functools

import jax
import jax.numpy as jnp
from jax import lax
from jax.experimental import pallas as pl
from jax.experimental.pallas import tpu as pltpu
from jax.sharding import Mesh, PartitionSpec as P

ITERS = 2
LANES = 128
HALF = LANES // 2
SLAB = 2
CHUNK = 16
VMEM = pl.BlockSpec(memory_space=pltpu.VMEM)


def split(x):
    high = x.astype(jnp.bfloat16)
    return high, (x - high.astype(jnp.float32)).astype(jnp.bfloat16)


def blocks(order):
    count = order // LANES
    return [(i, j) for i in range(count) for j in range(i + 1, count)]


def depth_of(order):
    return len(blocks(order)) * LANES + order // LANES * HALF * 3 // 2


def gram_kernel(scale, cores, chips, wide_ref, out_ref):
    high, low = split(wide_ref[...])
    order = high.shape[0]
    half = order // 2
    dims = (((1,), (1,)), ((), ()))
    dot = functools.partial(lax.dot_general, dimension_numbers=dims, preferred_element_type=jnp.float32)
    parts = {}
    for i in range(2):
        for j in range(i, 2):
            a, b = slice(i * half, (i + 1) * half), slice(j * half, (j + 1) * half)
            parts[i, j] = dot(high[a], high[b]) + (dot(high[a], low[b]) + dot(low[a], high[b]))
    per = half // LANES
    share = out_ref.shape[0] // (cores * chips)
    row = 0

    def block(i, j):
        r, c = (i % per) * LANES, (j % per) * LANES
        return parts[i // per, j // per][r : r + LANES, c : c + LANES] * scale

    def store(row, value):
        for at in range(0, value.shape[0], CHUNK):
            group, inside = divmod(row + at, share)
            core, chip = divmod(group, chips)
            to = (chip * cores + core) * share + inside
            out_ref[to : to + CHUNK, :] = value[at : at + CHUNK]
        return row + value.shape[0]

    for i, j in blocks(order):
        row = store(row, block(i, j))
    for i in range(0, order // LANES, 2):
        first, second = block(i, i), block(i + 1, i + 1)
        row = store(row, first[:HALF])
        row = store(row, second[:HALF])
        row = store(row, jnp.concatenate([first[HALF:, HALF:], second[HALF:, HALF:]], axis=1))


def unpack(gram_ref, full_ref):
    order = full_ref.shape[0]
    row = 0
    for i, j in blocks(order):
        part = gram_ref[row : row + LANES, :]
        full_ref[i * LANES : (i + 1) * LANES, j * LANES : (j + 1) * LANES] = part
        full_ref[j * LANES : (j + 1) * LANES, i * LANES : (i + 1) * LANES] = part.T
        row += LANES
    for i in range(0, order // LANES, 2):
        ends = gram_ref[row + LANES : row + LANES + HALF, :]
        for k in range(2):
            at = (i + k) * LANES
            top = gram_ref[row + k * HALF : row + (k + 1) * HALF, :]
            bottom = [top[:, HALF:].T, ends[:, k * HALF : (k + 1) * HALF]]
            full_ref[at : at + HALF, at : at + LANES] = top
            full_ref[at + HALF : at + LANES, at : at + LANES] = jnp.concatenate(bottom, axis=1)
        row += LANES + HALF


def inverse_factor(work, column_ref):
    n = work.shape[0]
    shape = (8, 2 * n)
    panels = n // 8
    tiles = [work[8 * k : 8 * k + 8] for k in range(panels)]
    sub = lax.broadcasted_iota(jnp.int32, shape, 0)
    done = []
    for p in range(panels):
        at = n + 8 * p
        rest = range(p + 1, panels)

        def column(tile, j):
            return jnp.broadcast_to(tile[:, at + j : at + j + 1], shape)

        for j in range(8):
            column_ref[p, j] = column(tiles[p], j)
        rows = [jnp.broadcast_to(tiles[p][i : i + 1], shape) for i in range(8)]
        pivot = {
            (i, j): jnp.broadcast_to(column_ref[p, j, i : i + 1, :], shape)
            for j in range(8)
            for i in range(j, 8)
        }
        below = {t: [column(tiles[t], j) for j in range(8)] for t in rest}
        factor, scaled = {}, []
        for i in range(8):
            inverse = 1.0 / pivot[i, i]
            scaled.append(rows[i] * inverse)
            for j in range(i + 1, 8):
                factor[j, i] = pivot[j, i] * inverse
            for j in range(i + 1, 8):
                for m in range(i + 1, j + 1):
                    pivot[j, m] = pivot[j, m] - factor[j, i] * pivot[m, i]
                rows[j] = rows[j] - factor[j, i] * rows[i]
            for t in rest:
                tiles[t] = tiles[t] - below[t][i] * scaled[i]
                for j in range(i + 1, 8):
                    below[t][j] = below[t][j] - factor[j, i] * below[t][i]
        final = rows[0] * lax.rsqrt(pivot[0, 0])
        for i in range(1, 8):
            final = jnp.where(sub == i, rows[i] * lax.rsqrt(pivot[i, i]), final)
        done.append(final)
    return jnp.concatenate(done, axis=0)[:, :n]


def core_kernel(gram_ref, start_ref, wide_ref, out_ref, full_ref, column_ref):
    unpack(gram_ref, full_ref)
    dot = functools.partial(
        lax.dot_general, precision=lax.Precision.HIGHEST, preferred_element_type=jnp.float32
    )
    plain, across = (((1,), (0,)), ((), ())), (((1,), (1,)), ((), ()))
    rank = start_ref.shape[0]
    shape = (rank, 2 * rank)
    row, lane = (lax.broadcasted_iota(jnp.int32, shape, axis) for axis in (0, 1))
    eye = (row == lane).astype(jnp.float32)
    image = dot(start_ref[...], full_ref[...], plain)
    for step in range(ITERS):
        small = dot(image, jnp.concatenate([jnp.zeros_like(image), image], axis=0), across)
        follow = dot(image, full_ref[...] if step + 1 < ITERS else wide_ref[...], plain)
        image = dot(inverse_factor(small + eye, column_ref), follow, plain)
    out_ref[...] = image


def exchange(x, axes):
    return lax.all_to_all(x, axes, 0, 0, tiled=True)


def added(pieces, count):
    return jnp.sum(pieces.reshape(count, pieces.shape[0] // count, *pieces.shape[1:]), axis=0)


def spread(block, count):
    copies = jnp.broadcast_to(block, (count, *block.shape))
    return copies.reshape(count * block.shape[0], *block.shape[1:])


def shards(count, group_axes, all_axes, core_axes, plane_axes, line_axes, field, start):
    groups = lax.axis_size(group_axes)
    times, species, rows, planes = field.shape
    moments = times * species
    order, rank = start.shape
    params = pltpu.CompilerParams(vmem_limit_bytes=40 * 1024 * 1024)

    wide = exchange(field.reshape(moments, rows, planes), group_axes)
    wide = wide.reshape(groups, moments // groups, rows, planes)
    wide = jnp.moveaxis(wide, 1, 2).reshape(order, moments // groups * planes)

    depth = depth_of(order)
    cores = lax.axis_size(core_axes)
    partial_gram = pl.pallas_call(
        functools.partial(gram_kernel, 1.0 / count, cores, groups // cores),
        in_specs=[VMEM],
        out_specs=VMEM,
        out_shape=jax.ShapeDtypeStruct((depth, LANES), jnp.float32),
        compiler_params=params,
    )(wide)

    gram = partial_gram.reshape(depth // SLAB, SLAB, LANES)
    gram = added(exchange(gram, all_axes), lax.axis_size(all_axes))
    line = lax.axis_size(line_axes)
    gram = added(exchange(spread(gram, line), line_axes), line)
    for axes in (plane_axes, core_axes):
        gram = exchange(spread(gram, lax.axis_size(axes)), axes)
    gram = gram.reshape(depth, LANES)

    plane_core = pl.pallas_call(
        core_kernel,
        in_specs=[VMEM] * 3,
        out_specs=VMEM,
        out_shape=jax.ShapeDtypeStruct((rank, wide.shape[1]), jnp.float32),
        scratch_shapes=[
            pltpu.VMEM((order, order), jnp.float32),
            pltpu.VMEM((rank // 8, 8, 8, 2 * rank), jnp.float32),
        ],
        compiler_params=params,
    )(gram, start.T, wide)
    plane_core = plane_core.reshape(rank, moments // groups, planes)
    plane_core = plane_core.reshape(groups, rank // groups, moments // groups, planes)
    core = exchange(jnp.moveaxis(plane_core, 2, 1).reshape(moments, rank // groups, planes), group_axes)
    return core.reshape(times, species, rank // groups, planes)


def solution(mesh):
    fine = Mesh(
        mesh.devices.reshape(4, 2, 4, 2, 4, 2), ("y", "core", "z_mid", "z_pair", "x", "z_hi")
    )
    placed = P("z_hi", None, ("y", "core"), ("z_mid", "z_pair", "x"))

    def program(field, start):
        count = field.shape[0] * field.shape[1] * field.shape[3]
        body = functools.partial(
            shards,
            count,
            ("y", "core"),
            ("y", "core", "z_pair", "x"),
            "core",
            ("y", "z_pair", "x"),
            ("z_mid", "z_hi"),
        )
        return jax.shard_map(
            body, mesh=fine, in_specs=(placed, P()), out_specs=placed, check_vma=False
        )(field, start)

    return program
```

```python
import functools

import jax
import jax.numpy as jnp
from jax import lax
from jax.experimental import pallas as pl
from jax.experimental.pallas import tpu as pltpu
from jax.sharding import Mesh, PartitionSpec as P

ITERS = 2
LANES = 128
HALF = LANES // 2
SLAB = 2
CHUNK = 16
VMEM = pl.BlockSpec(memory_space=pltpu.VMEM)


def split(x):
    high = x.astype(jnp.bfloat16)
    return high, (x - high.astype(jnp.float32)).astype(jnp.bfloat16)


def blocks(order):
    count = order // LANES
    return [(i, j) for i in range(count) for j in range(i + 1, count)]


def depth_of(order):
    return len(blocks(order)) * LANES + order // LANES * HALF * 3 // 2


def gram_kernel(scale, cores, chips, wide_ref, out_ref):
    high, low = split(wide_ref[...])
    order = high.shape[0]
    half = order // 2
    dims = (((1,), (1,)), ((), ()))
    dot = functools.partial(lax.dot_general, dimension_numbers=dims, preferred_element_type=jnp.float32)
    parts = {}
    for i in range(2):
        for j in range(i, 2):
            a, b = slice(i * half, (i + 1) * half), slice(j * half, (j + 1) * half)
            parts[i, j] = dot(high[a], high[b]) + (dot(high[a], low[b]) + dot(low[a], high[b]))
    per = half // LANES
    share = out_ref.shape[0] // (cores * chips)
    row = 0

    def block(i, j):
        r, c = (i % per) * LANES, (j % per) * LANES
        return parts[i // per, j // per][r : r + LANES, c : c + LANES] * scale

    def store(row, value):
        for at in range(0, value.shape[0], CHUNK):
            group, inside = divmod(row + at, share)
            core, chip = divmod(group, chips)
            to = (chip * cores + core) * share + inside
            out_ref[to : to + CHUNK, :] = value[at : at + CHUNK]
        return row + value.shape[0]

    for i, j in blocks(order):
        row = store(row, block(i, j))
    for i in range(0, order // LANES, 2):
        first, second = block(i, i), block(i + 1, i + 1)
        row = store(row, first[:HALF])
        row = store(row, second[:HALF])
        row = store(row, jnp.concatenate([first[HALF:, HALF:], second[HALF:, HALF:]], axis=1))


def unpack(gram_ref, full_ref):
    order = full_ref.shape[0]
    row = 0
    for i, j in blocks(order):
        part = gram_ref[row : row + LANES, :]
        full_ref[i * LANES : (i + 1) * LANES, j * LANES : (j + 1) * LANES] = part
        full_ref[j * LANES : (j + 1) * LANES, i * LANES : (i + 1) * LANES] = part.T
        row += LANES
    for i in range(0, order // LANES, 2):
        ends = gram_ref[row + LANES : row + LANES + HALF, :]
        for k in range(2):
            at = (i + k) * LANES
            top = gram_ref[row + k * HALF : row + (k + 1) * HALF, :]
            bottom = [top[:, HALF:].T, ends[:, k * HALF : (k + 1) * HALF]]
            full_ref[at : at + HALF, at : at + LANES] = top
            full_ref[at + HALF : at + LANES, at : at + LANES] = jnp.concatenate(bottom, axis=1)
        row += LANES + HALF


def inverse_factor(work, column_ref):
    n = work.shape[0]
    shape = (8, 2 * n)
    panels = n // 8
    tiles = [work[8 * k : 8 * k + 8] for k in range(panels)]
    sub = lax.broadcasted_iota(jnp.int32, shape, 0)
    done = []
    for p in range(panels):
        at = n + 8 * p
        rest = range(p + 1, panels)

        def column(tile, j):
            return jnp.broadcast_to(tile[:, at + j : at + j + 1], shape)

        for j in range(8):
            column_ref[p, j] = column(tiles[p], j)
        rows = [jnp.broadcast_to(tiles[p][i : i + 1], shape) for i in range(8)]
        pivot = {
            (i, j): jnp.broadcast_to(column_ref[p, j, i : i + 1, :], shape)
            for j in range(8)
            for i in range(j, 8)
        }
        below = {t: [column(tiles[t], j) for j in range(8)] for t in rest}
        factor, scaled = {}, []
        for i in range(8):
            inverse = 1.0 / pivot[i, i]
            scaled.append(rows[i] * inverse)
            for j in range(i + 1, 8):
                factor[j, i] = pivot[j, i] * inverse
            for j in range(i + 1, 8):
                for m in range(i + 1, j + 1):
                    pivot[j, m] = pivot[j, m] - factor[j, i] * pivot[m, i]
                rows[j] = rows[j] - factor[j, i] * rows[i]
            for t in rest:
                tiles[t] = tiles[t] - below[t][i] * scaled[i]
                for j in range(i + 1, 8):
                    below[t][j] = below[t][j] - factor[j, i] * below[t][i]
        final = rows[0] * lax.rsqrt(pivot[0, 0])
        for i in range(1, 8):
            final = jnp.where(sub == i, rows[i] * lax.rsqrt(pivot[i, i]), final)
        done.append(final)
    return jnp.concatenate(done, axis=0)[:, :n]


def core_kernel(place_ref, mine_ref, other_ref, start_ref, wide_ref, out_ref, gram_ref, full_ref, column_ref):
    size = mine_ref.shape[0]
    for part_ref, place in ((mine_ref, place_ref[0]), (other_ref, 1 - place_ref[0])):
        gram_ref[pl.ds(pl.multiple_of(place * size, 8), size), :] = part_ref[...]
    unpack(gram_ref, full_ref)
    dot = functools.partial(
        lax.dot_general, precision=lax.Precision.HIGHEST, preferred_element_type=jnp.float32
    )
    plain, across = (((1,), (0,)), ((), ())), (((1,), (1,)), ((), ()))
    rank = start_ref.shape[0]
    shape = (rank, 2 * rank)
    row, lane = (lax.broadcasted_iota(jnp.int32, shape, axis) for axis in (0, 1))
    eye = (row == lane).astype(jnp.float32)
    image = dot(start_ref[...], full_ref[...], plain)
    for step in range(ITERS):
        small = dot(image, jnp.concatenate([jnp.zeros_like(image), image], axis=0), across)
        follow = dot(image, full_ref[...] if step + 1 < ITERS else wide_ref[...], plain)
        image = dot(inverse_factor(small + eye, column_ref), follow, plain)
    out_ref[...] = image


def exchange(x, axes):
    return lax.all_to_all(x, axes, 0, 0, tiled=True)


def added(pieces, count):
    return jnp.sum(pieces.reshape(count, pieces.shape[0] // count, *pieces.shape[1:]), axis=0)


def spread(block, count):
    copies = jnp.broadcast_to(block, (count, *block.shape))
    return copies.reshape(count * block.shape[0], *block.shape[1:])


def shards(count, group_axes, all_axes, core_axes, plane_axes, line_axes, field, start):
    groups = lax.axis_size(group_axes)
    times, species, rows, planes = field.shape
    moments = times * species
    order, rank = start.shape
    params = pltpu.CompilerParams(vmem_limit_bytes=40 * 1024 * 1024)

    wide = exchange(field.reshape(moments, rows, planes), group_axes)
    wide = wide.reshape(groups, moments // groups, rows, planes)
    wide = jnp.moveaxis(wide, 1, 2).reshape(order, moments // groups * planes)

    depth = depth_of(order)
    cores = lax.axis_size(core_axes)
    partial_gram = pl.pallas_call(
        functools.partial(gram_kernel, 1.0 / count, cores, groups // cores),
        in_specs=[VMEM],
        out_specs=VMEM,
        out_shape=jax.ShapeDtypeStruct((depth, LANES), jnp.float32),
        compiler_params=params,
    )(wide)

    gram = partial_gram.reshape(depth // SLAB, SLAB, LANES)
    gram = added(exchange(gram, all_axes), lax.axis_size(all_axes))
    line = lax.axis_size(line_axes)
    gram = added(exchange(spread(gram, line), line_axes), line)
    mine = exchange(spread(gram, lax.axis_size(plane_axes)), plane_axes)
    mine = mine.reshape(depth // cores, LANES)
    other = lax.ppermute(mine, core_axes, [(0, 1), (1, 0)])
    place = lax.axis_index(core_axes).astype(jnp.int32).reshape(1)

    plane_core = pl.pallas_call(
        core_kernel,
        in_specs=[pl.BlockSpec(memory_space=pltpu.SMEM)] + [VMEM] * 4,
        out_specs=VMEM,
        out_shape=jax.ShapeDtypeStruct((rank, wide.shape[1]), jnp.float32),
        scratch_shapes=[
            pltpu.VMEM((depth, LANES), jnp.float32),
            pltpu.VMEM((order, order), jnp.float32),
            pltpu.VMEM((rank // 8, 8, 8, 2 * rank), jnp.float32),
        ],
        compiler_params=params,
    )(place, mine, other, start.T, wide)
    plane_core = plane_core.reshape(rank, moments // groups, planes)
    plane_core = plane_core.reshape(groups, rank // groups, moments // groups, planes)
    core = exchange(jnp.moveaxis(plane_core, 2, 1).reshape(moments, rank // groups, planes), group_axes)
    return core.reshape(times, species, rank // groups, planes)


def solution(mesh):
    fine = Mesh(
        mesh.devices.reshape(4, 2, 4, 2, 4, 2), ("y", "core", "z_mid", "z_pair", "x", "z_hi")
    )
    placed = P("z_hi", None, ("y", "core"), ("z_mid", "z_pair", "x"))

    def program(field, start):
        count = field.shape[0] * field.shape[1] * field.shape[3]
        body = functools.partial(
            shards,
            count,
            ("y", "core"),
            ("y", "core", "z_pair", "x"),
            "core",
            ("y", "z_pair", "x"),
            ("z_mid", "z_hi"),
        )
        return jax.shard_map(
            body, mesh=fine, in_specs=(placed, P()), out_specs=placed, check_vma=False
        )(field, start)

    return program
```

```python
import functools

import jax
import jax.numpy as jnp
from jax import lax
from jax.experimental import pallas as pl
from jax.experimental.pallas import tpu as pltpu
from jax.sharding import Mesh, PartitionSpec as P

ITERS = 2
LANES = 128
HALF = LANES // 2
SLAB = 2
VMEM = pl.BlockSpec(memory_space=pltpu.VMEM)


def split(x):
    high = x.astype(jnp.bfloat16)
    return high, (x - high.astype(jnp.float32)).astype(jnp.bfloat16)


def blocks(order):
    count = order // LANES
    return [(i, j) for i in range(count) for j in range(i + 1, count)]


def depth_of(order):
    return len(blocks(order)) * LANES + order // LANES * HALF * 3 // 2


def gram_kernel(scale, place_ref, wide_ref, keep_ref, send_ref, packed_ref):
    high, low = split(wide_ref[...])
    order = high.shape[0]
    half = order // 2
    dims = (((1,), (1,)), ((), ()))
    dot = functools.partial(lax.dot_general, dimension_numbers=dims, preferred_element_type=jnp.float32)
    parts = {}
    for i in range(2):
        for j in range(i, 2):
            a, b = slice(i * half, (i + 1) * half), slice(j * half, (j + 1) * half)
            parts[i, j] = dot(high[a], high[b]) + (dot(high[a], low[b]) + dot(low[a], high[b]))
    per = half // LANES
    row = 0

    def block(i, j):
        r, c = (i % per) * LANES, (j % per) * LANES
        return parts[i // per, j // per][r : r + LANES, c : c + LANES] * scale

    def store(row, value):
        packed_ref[row : row + value.shape[0], :] = value
        return row + value.shape[0]

    for i, j in blocks(order):
        row = store(row, block(i, j))
    for i in range(0, order // LANES, 2):
        first, second = block(i, i), block(i + 1, i + 1)
        row = store(row, first[:HALF])
        row = store(row, second[:HALF])
        row = store(row, jnp.concatenate([first[HALF:, HALF:], second[HALF:, HALF:]], axis=1))
    size = keep_ref.shape[0]
    for part_ref, place in ((keep_ref, place_ref[0]), (send_ref, 1 - place_ref[0])):
        part_ref[...] = packed_ref[pl.ds(pl.multiple_of(place * size, 8), size), :]


def unpack(gram_ref, full_ref):
    order = full_ref.shape[0]
    row = 0
    for i, j in blocks(order):
        part = gram_ref[row : row + LANES, :]
        full_ref[i * LANES : (i + 1) * LANES, j * LANES : (j + 1) * LANES] = part
        full_ref[j * LANES : (j + 1) * LANES, i * LANES : (i + 1) * LANES] = part.T
        row += LANES
    for i in range(0, order // LANES, 2):
        ends = gram_ref[row + LANES : row + LANES + HALF, :]
        for k in range(2):
            at = (i + k) * LANES
            top = gram_ref[row + k * HALF : row + (k + 1) * HALF, :]
            bottom = [top[:, HALF:].T, ends[:, k * HALF : (k + 1) * HALF]]
            full_ref[at : at + HALF, at : at + LANES] = top
            full_ref[at + HALF : at + LANES, at : at + LANES] = jnp.concatenate(bottom, axis=1)
        row += LANES + HALF


def inverse_factor(work, column_ref):
    n = work.shape[0]
    shape = (8, 2 * n)
    panels = n // 8
    tiles = [work[8 * k : 8 * k + 8] for k in range(panels)]
    sub = lax.broadcasted_iota(jnp.int32, shape, 0)
    done = []
    for p in range(panels):
        at = n + 8 * p
        rest = range(p + 1, panels)

        def column(tile, j):
            return jnp.broadcast_to(tile[:, at + j : at + j + 1], shape)

        for j in range(8):
            column_ref[p, j] = column(tiles[p], j)
        rows = [jnp.broadcast_to(tiles[p][i : i + 1], shape) for i in range(8)]
        pivot = {
            (i, j): jnp.broadcast_to(column_ref[p, j, i : i + 1, :], shape)
            for j in range(8)
            for i in range(j, 8)
        }
        below = {t: [column(tiles[t], j) for j in range(8)] for t in rest}
        factor, scaled = {}, []
        for i in range(8):
            inverse = 1.0 / pivot[i, i]
            scaled.append(rows[i] * inverse)
            for j in range(i + 1, 8):
                factor[j, i] = pivot[j, i] * inverse
            for j in range(i + 1, 8):
                for m in range(i + 1, j + 1):
                    pivot[j, m] = pivot[j, m] - factor[j, i] * pivot[m, i]
                rows[j] = rows[j] - factor[j, i] * rows[i]
            for t in rest:
                tiles[t] = tiles[t] - below[t][i] * scaled[i]
                for j in range(i + 1, 8):
                    below[t][j] = below[t][j] - factor[j, i] * below[t][i]
        final = rows[0] * lax.rsqrt(pivot[0, 0])
        for i in range(1, 8):
            final = jnp.where(sub == i, rows[i] * lax.rsqrt(pivot[i, i]), final)
        done.append(final)
    return jnp.concatenate(done, axis=0)[:, :n]


def core_kernel(place_ref, mine_ref, other_ref, start_ref, wide_ref, out_ref, gram_ref, full_ref, column_ref):
    size = mine_ref.shape[0]
    for part_ref, place in ((mine_ref, place_ref[0]), (other_ref, 1 - place_ref[0])):
        gram_ref[pl.ds(pl.multiple_of(place * size, 8), size), :] = part_ref[...]
    unpack(gram_ref, full_ref)
    dot = functools.partial(
        lax.dot_general, precision=lax.Precision.HIGHEST, preferred_element_type=jnp.float32
    )
    plain, across = (((1,), (0,)), ((), ())), (((1,), (1,)), ((), ()))
    rank = start_ref.shape[0]
    shape = (rank, 2 * rank)
    row, lane = (lax.broadcasted_iota(jnp.int32, shape, axis) for axis in (0, 1))
    eye = (row == lane).astype(jnp.float32)
    image = dot(start_ref[...], full_ref[...], plain)
    for step in range(ITERS):
        small = dot(image, jnp.concatenate([jnp.zeros_like(image), image], axis=0), across)
        follow = dot(image, full_ref[...] if step + 1 < ITERS else wide_ref[...], plain)
        image = dot(inverse_factor(small + eye, column_ref), follow, plain)
    out_ref[...] = image


def exchange(x, axes):
    return lax.all_to_all(x, axes, 0, 0, tiled=True)


def added(pieces, count):
    return jnp.sum(pieces.reshape(count, pieces.shape[0] // count, *pieces.shape[1:]), axis=0)


def spread(block, count):
    copies = jnp.broadcast_to(block, (count, *block.shape))
    return copies.reshape(count * block.shape[0], *block.shape[1:])


def shards(count, group_axes, core_axes, plane_axes, line_axes, field, start):
    groups = lax.axis_size(group_axes)
    times, species, rows, planes = field.shape
    moments = times * species
    order, rank = start.shape
    params = pltpu.CompilerParams(vmem_limit_bytes=40 * 1024 * 1024)

    wide = exchange(field.reshape(moments, rows, planes), group_axes)
    wide = wide.reshape(groups, moments // groups, rows, planes)
    wide = jnp.moveaxis(wide, 1, 2).reshape(order, moments // groups * planes)

    depth = depth_of(order)
    cores = lax.axis_size(core_axes)
    half = jax.ShapeDtypeStruct((depth // cores, LANES), jnp.float32)
    place = lax.axis_index(core_axes).astype(jnp.int32).reshape(1)
    scalar = pl.BlockSpec(memory_space=pltpu.SMEM)
    keep, send = pl.pallas_call(
        functools.partial(gram_kernel, 1.0 / count),
        in_specs=[scalar, VMEM],
        out_specs=[VMEM] * 2,
        out_shape=[half] * 2,
        scratch_shapes=[pltpu.VMEM((depth, LANES), jnp.float32)],
        compiler_params=params,
    )(place, wide)

    swap = functools.partial(lax.ppermute, axis_name=core_axes, perm=[(0, 1), (1, 0)])
    gram = (keep + swap(send)).reshape(depth // cores // SLAB, SLAB, LANES)
    gram = added(exchange(gram, plane_axes), lax.axis_size(plane_axes))
    line = lax.axis_size(line_axes)
    gram = added(exchange(spread(gram, line), line_axes), line)
    mine = exchange(spread(gram, lax.axis_size(plane_axes)), plane_axes)
    mine = mine.reshape(depth // cores, LANES)
    other = swap(mine)

    plane_core = pl.pallas_call(
        core_kernel,
        in_specs=[scalar] + [VMEM] * 4,
        out_specs=VMEM,
        out_shape=jax.ShapeDtypeStruct((rank, wide.shape[1]), jnp.float32),
        scratch_shapes=[
            pltpu.VMEM((depth, LANES), jnp.float32),
            pltpu.VMEM((order, order), jnp.float32),
            pltpu.VMEM((rank // 8, 8, 8, 2 * rank), jnp.float32),
        ],
        compiler_params=params,
    )(place, mine, other, start.T, wide)
    plane_core = plane_core.reshape(rank, moments // groups, planes)
    plane_core = plane_core.reshape(groups, rank // groups, moments // groups, planes)
    core = exchange(jnp.moveaxis(plane_core, 2, 1).reshape(moments, rank // groups, planes), group_axes)
    return core.reshape(times, species, rank // groups, planes)


def solution(mesh):
    fine = Mesh(
        mesh.devices.reshape(4, 2, 4, 2, 4, 2), ("y", "core", "z_mid", "z_pair", "x", "z_hi")
    )
    placed = P("z_hi", None, ("y", "core"), ("z_mid", "z_pair", "x"))

    def program(field, start):
        count = field.shape[0] * field.shape[1] * field.shape[3]
        body = functools.partial(
            shards,
            count,
            ("y", "core"),
            "core",
            ("y", "z_pair", "x"),
            ("z_mid", "z_hi"),
        )
        return jax.shard_map(
            body, mesh=fine, in_specs=(placed, P()), out_specs=placed, check_vma=False
        )(field, start)

    return program
```

```python
import functools

import jax
import jax.numpy as jnp
from jax import lax
from jax.experimental import pallas as pl
from jax.experimental.pallas import tpu as pltpu
from jax.sharding import Mesh, PartitionSpec as P

ITERS = 2
LANES = 128
HALF = LANES // 2
SLAB = 2
VMEM = pl.BlockSpec(memory_space=pltpu.VMEM)


def split(x):
    high = x.astype(jnp.bfloat16)
    return high, (x - high.astype(jnp.float32)).astype(jnp.bfloat16)


def blocks(order):
    count = order // LANES
    return [(i, j) for i in range(count) for j in range(i + 1, count)]


def depth_of(order):
    return len(blocks(order)) * LANES + order // LANES * HALF * 3 // 2


def gram_kernel(scale, place_ref, wide_ref, keep_ref, send_ref, packed_ref):
    high, low = split(wide_ref[...])
    order = high.shape[0]
    half = order // 2
    dims = (((1,), (1,)), ((), ()))
    dot = functools.partial(lax.dot_general, dimension_numbers=dims, preferred_element_type=jnp.float32)
    parts = {}
    for i in range(2):
        for j in range(i, 2):
            a, b = slice(i * half, (i + 1) * half), slice(j * half, (j + 1) * half)
            parts[i, j] = dot(high[a], high[b]) + (dot(high[a], low[b]) + dot(low[a], high[b]))
    per = half // LANES
    row = 0

    def block(i, j):
        r, c = (i % per) * LANES, (j % per) * LANES
        return parts[i // per, j // per][r : r + LANES, c : c + LANES] * scale

    def store(row, value):
        packed_ref[row : row + value.shape[0], :] = value
        return row + value.shape[0]

    for i, j in blocks(order):
        row = store(row, block(i, j))
    for i in range(0, order // LANES, 2):
        first, second = block(i, i), block(i + 1, i + 1)
        row = store(row, first[:HALF])
        row = store(row, second[:HALF])
        row = store(row, jnp.concatenate([first[HALF:, HALF:], second[HALF:, HALF:]], axis=1))
    size = keep_ref.shape[0]
    for part_ref, place in ((keep_ref, place_ref[0]), (send_ref, 1 - place_ref[0])):
        part_ref[...] = packed_ref[pl.ds(pl.multiple_of(place * size, 8), size), :]


def unpack(gram_ref, full_ref):
    order = full_ref.shape[0]
    row = 0
    for i, j in blocks(order):
        part = gram_ref[row : row + LANES, :]
        full_ref[i * LANES : (i + 1) * LANES, j * LANES : (j + 1) * LANES] = part
        full_ref[j * LANES : (j + 1) * LANES, i * LANES : (i + 1) * LANES] = part.T
        row += LANES
    for i in range(0, order // LANES, 2):
        ends = gram_ref[row + LANES : row + LANES + HALF, :]
        for k in range(2):
            at = (i + k) * LANES
            top = gram_ref[row + k * HALF : row + (k + 1) * HALF, :]
            bottom = [top[:, HALF:].T, ends[:, k * HALF : (k + 1) * HALF]]
            full_ref[at : at + HALF, at : at + LANES] = top
            full_ref[at + HALF : at + LANES, at : at + LANES] = jnp.concatenate(bottom, axis=1)
        row += LANES + HALF


def inverse_factor(work, column_ref, near_ref):
    n = work.shape[0]
    shape = (8, 2 * n)
    panels = n // 8
    tiles = [work[8 * k : 8 * k + 8] for k in range(panels)]
    sub = lax.broadcasted_iota(jnp.int32, shape, 0)
    done = []
    ready = None
    for p in range(panels):
        at = n + 8 * p
        rest = range(p + 1, panels)

        def column(tile, j):
            return jnp.broadcast_to(tile[:, at + j : at + j + 1], shape)

        for j in range(8):
            column_ref[p, j] = column(tiles[p], j) if ready is None else ready[j]
        ready = [column(tiles[p + 1], 8 + j) for j in range(8)] if rest else None
        rows = [jnp.broadcast_to(tiles[p][i : i + 1], shape) for i in range(8)]
        pivot = {
            (i, j): jnp.broadcast_to(column_ref[p, j, i : i + 1, :], shape)
            for j in range(8)
            for i in range(j, 8)
        }
        below = {t: [column(tiles[t], j) for j in range(8)] for t in rest}
        factor, scaled = {}, []
        for i in range(8):
            inverse = 1.0 / pivot[i, i]
            scaled.append(rows[i] * inverse)
            for j in range(i + 1, 8):
                factor[j, i] = pivot[j, i] * inverse
            for j in range(i + 1, 8):
                for m in range(i + 1, j + 1):
                    pivot[j, m] = pivot[j, m] - factor[j, i] * pivot[m, i]
                rows[j] = rows[j] - factor[j, i] * rows[i]
            if rest:
                near_ref[p, i] = below[p + 1][i]
                for j in range(8):
                    across = jnp.broadcast_to(near_ref[p, i, j : j + 1, :], shape)
                    ready[j] = ready[j] - below[p + 1][i] * (across * inverse)
            for t in rest:
                tiles[t] = tiles[t] - below[t][i] * scaled[i]
                for j in range(i + 1, 8):
                    below[t][j] = below[t][j] - factor[j, i] * below[t][i]
        final = rows[0] * lax.rsqrt(pivot[0, 0])
        for i in range(1, 8):
            final = jnp.where(sub == i, rows[i] * lax.rsqrt(pivot[i, i]), final)
        done.append(final)
    return jnp.concatenate(done, axis=0)[:, :n]


def core_kernel(place_ref, mine_ref, other_ref, start_ref, wide_ref, out_ref, gram_ref, full_ref, column_ref, near_ref):
    size = mine_ref.shape[0]
    for part_ref, place in ((mine_ref, place_ref[0]), (other_ref, 1 - place_ref[0])):
        gram_ref[pl.ds(pl.multiple_of(place * size, 8), size), :] = part_ref[...]
    unpack(gram_ref, full_ref)
    dot = functools.partial(
        lax.dot_general, precision=lax.Precision.HIGHEST, preferred_element_type=jnp.float32
    )
    plain, across = (((1,), (0,)), ((), ())), (((1,), (1,)), ((), ()))
    rank = start_ref.shape[0]
    shape = (rank, 2 * rank)
    row, lane = (lax.broadcasted_iota(jnp.int32, shape, axis) for axis in (0, 1))
    eye = (row == lane).astype(jnp.float32)
    image = dot(start_ref[...], full_ref[...], plain)
    for step in range(ITERS):
        small = dot(image, jnp.concatenate([jnp.zeros_like(image), image], axis=0), across)
        follow = dot(image, full_ref[...] if step + 1 < ITERS else wide_ref[...], plain)
        image = dot(inverse_factor(small + eye, column_ref, near_ref), follow, plain)
    out_ref[...] = image


def exchange(x, axes):
    return lax.all_to_all(x, axes, 0, 0, tiled=True)


def added(pieces, count):
    return jnp.sum(pieces.reshape(count, pieces.shape[0] // count, *pieces.shape[1:]), axis=0)


def spread(block, count):
    copies = jnp.broadcast_to(block, (count, *block.shape))
    return copies.reshape(count * block.shape[0], *block.shape[1:])


def shards(count, group_axes, core_axes, plane_axes, line_axes, field, start):
    groups = lax.axis_size(group_axes)
    times, species, rows, planes = field.shape
    moments = times * species
    order, rank = start.shape
    params = pltpu.CompilerParams(vmem_limit_bytes=40 * 1024 * 1024)

    wide = exchange(field.reshape(moments, rows, planes), group_axes)
    wide = wide.reshape(groups, moments // groups, rows, planes)
    wide = jnp.moveaxis(wide, 1, 2).reshape(order, moments // groups * planes)

    depth = depth_of(order)
    cores = lax.axis_size(core_axes)
    half = jax.ShapeDtypeStruct((depth // cores, LANES), jnp.float32)
    place = lax.axis_index(core_axes).astype(jnp.int32).reshape(1)
    scalar = pl.BlockSpec(memory_space=pltpu.SMEM)
    keep, send = pl.pallas_call(
        functools.partial(gram_kernel, 1.0 / count),
        in_specs=[scalar, VMEM],
        out_specs=[VMEM] * 2,
        out_shape=[half] * 2,
        scratch_shapes=[pltpu.VMEM((depth, LANES), jnp.float32)],
        compiler_params=params,
    )(place, wide)

    swap = functools.partial(lax.ppermute, axis_name=core_axes, perm=[(0, 1), (1, 0)])
    gram = (keep + swap(send)).reshape(depth // cores // SLAB, SLAB, LANES)
    gram = added(exchange(gram, plane_axes), lax.axis_size(plane_axes))
    line = lax.axis_size(line_axes)
    gram = added(exchange(spread(gram, line), line_axes), line)
    mine = exchange(spread(gram, lax.axis_size(plane_axes)), plane_axes)
    mine = mine.reshape(depth // cores, LANES)
    other = swap(mine)

    plane_core = pl.pallas_call(
        core_kernel,
        in_specs=[scalar] + [VMEM] * 4,
        out_specs=VMEM,
        out_shape=jax.ShapeDtypeStruct((rank, wide.shape[1]), jnp.float32),
        scratch_shapes=[
            pltpu.VMEM((depth, LANES), jnp.float32),
            pltpu.VMEM((order, order), jnp.float32),
            pltpu.VMEM((rank // 8, 8, 8, 2 * rank), jnp.float32),
            pltpu.VMEM((rank // 8, 8, 8, 2 * rank), jnp.float32),
        ],
        compiler_params=params,
    )(place, mine, other, start.T, wide)
    plane_core = plane_core.reshape(rank, moments // groups, planes)
    plane_core = plane_core.reshape(groups, rank // groups, moments // groups, planes)
    core = exchange(jnp.moveaxis(plane_core, 2, 1).reshape(moments, rank // groups, planes), group_axes)
    return core.reshape(times, species, rank // groups, planes)


def solution(mesh):
    fine = Mesh(
        mesh.devices.reshape(4, 2, 4, 2, 4, 2), ("y", "core", "z_mid", "z_pair", "x", "z_hi")
    )
    placed = P("z_hi", None, ("y", "core"), ("z_mid", "z_pair", "x"))

    def program(field, start):
        count = field.shape[0] * field.shape[1] * field.shape[3]
        body = functools.partial(
            shards,
            count,
            ("y", "core"),
            "core",
            ("y", "z_pair", "x"),
            ("z_mid", "z_hi"),
        )
        return jax.shard_map(
            body, mesh=fine, in_specs=(placed, P()), out_specs=placed, check_vma=False
        )(field, start)

    return program
```

```python
import functools

import jax
import jax.numpy as jnp
from jax import lax
from jax.experimental import pallas as pl
from jax.experimental.pallas import tpu as pltpu
from jax.sharding import Mesh, PartitionSpec as P

ITERS = 2
LANES = 128
HALF = LANES // 2
SLAB = 2
VMEM = pl.BlockSpec(memory_space=pltpu.VMEM)


def split(x):
    high = x.astype(jnp.bfloat16)
    return high, (x - high.astype(jnp.float32)).astype(jnp.bfloat16)


def blocks(order):
    count = order // LANES
    return [(i, j) for i in range(count) for j in range(i + 1, count)]


def depth_of(order):
    return len(blocks(order)) * LANES + order // LANES * HALF * 3 // 2


def gram_kernel(scale, place_ref, wide_ref, keep_ref, send_ref, packed_ref):
    high, low = split(wide_ref[...])
    order = high.shape[0]
    half = order // 2
    dims = (((1,), (1,)), ((), ()))
    dot = functools.partial(lax.dot_general, dimension_numbers=dims, preferred_element_type=jnp.float32)
    parts = {}
    for i in range(2):
        for j in range(i, 2):
            a, b = slice(i * half, (i + 1) * half), slice(j * half, (j + 1) * half)
            mixed = dot(high[a], low[b])
            mirror = mixed.T if i == j else dot(low[a], high[b])
            parts[i, j] = dot(high[a], high[b]) + (mixed + mirror)
    per = half // LANES
    row = 0

    def block(i, j):
        r, c = (i % per) * LANES, (j % per) * LANES
        return parts[i // per, j // per][r : r + LANES, c : c + LANES] * scale

    def store(row, value):
        packed_ref[row : row + value.shape[0], :] = value
        return row + value.shape[0]

    for i, j in blocks(order):
        row = store(row, block(i, j))
    for i in range(0, order // LANES, 2):
        first, second = block(i, i), block(i + 1, i + 1)
        row = store(row, first[:HALF])
        row = store(row, second[:HALF])
        row = store(row, jnp.concatenate([first[HALF:, HALF:], second[HALF:, HALF:]], axis=1))
    size = keep_ref.shape[0]
    for part_ref, place in ((keep_ref, place_ref[0]), (send_ref, 1 - place_ref[0])):
        part_ref[...] = packed_ref[pl.ds(pl.multiple_of(place * size, 8), size), :]


def unpack(gram_ref, full_ref):
    order = full_ref.shape[0]
    row = 0
    for i, j in blocks(order):
        part = gram_ref[row : row + LANES, :]
        full_ref[i * LANES : (i + 1) * LANES, j * LANES : (j + 1) * LANES] = part
        full_ref[j * LANES : (j + 1) * LANES, i * LANES : (i + 1) * LANES] = part.T
        row += LANES
    for i in range(0, order // LANES, 2):
        ends = gram_ref[row + LANES : row + LANES + HALF, :]
        for k in range(2):
            at = (i + k) * LANES
            top = gram_ref[row + k * HALF : row + (k + 1) * HALF, :]
            bottom = [top[:, HALF:].T, ends[:, k * HALF : (k + 1) * HALF]]
            full_ref[at : at + HALF, at : at + LANES] = top
            full_ref[at + HALF : at + LANES, at : at + LANES] = jnp.concatenate(bottom, axis=1)
        row += LANES + HALF


def inverse_factor(work, column_ref, near_ref):
    n = work.shape[0]
    shape = (8, 2 * n)
    panels = n // 8
    tiles = [work[8 * k : 8 * k + 8] for k in range(panels)]
    sub = lax.broadcasted_iota(jnp.int32, shape, 0)
    done = []
    ready = None
    for p in range(panels):
        at = n + 8 * p
        rest = range(p + 1, panels)

        def column(tile, j):
            return jnp.broadcast_to(tile[:, at + j : at + j + 1], shape)

        for j in range(8):
            column_ref[p, j] = column(tiles[p], j) if ready is None else ready[j]
        ready = [column(tiles[p + 1], 8 + j) for j in range(8)] if rest else None
        rows = [jnp.broadcast_to(tiles[p][i : i + 1], shape) for i in range(8)]
        pivot = {
            (i, j): jnp.broadcast_to(column_ref[p, j, i : i + 1, :], shape)
            for j in range(8)
            for i in range(j, 8)
        }
        below = {t: [column(tiles[t], j) for j in range(8)] for t in rest}
        factor, scaled = {}, []
        for i in range(8):
            inverse = 1.0 / pivot[i, i]
            scaled.append(rows[i] * inverse)
            for j in range(i + 1, 8):
                factor[j, i] = pivot[j, i] * inverse
            for j in range(i + 1, 8):
                for m in range(i + 1, j + 1):
                    pivot[j, m] = pivot[j, m] - factor[j, i] * pivot[m, i]
                rows[j] = rows[j] - factor[j, i] * rows[i]
            if rest:
                near_ref[p, i] = below[p + 1][i]
                for j in range(8):
                    across = jnp.broadcast_to(near_ref[p, i, j : j + 1, :], shape)
                    ready[j] = ready[j] - below[p + 1][i] * (across * inverse)
            for t in rest:
                tiles[t] = tiles[t] - below[t][i] * scaled[i]
                for j in range(i + 1, 8):
                    below[t][j] = below[t][j] - factor[j, i] * below[t][i]
        final = rows[0] * lax.rsqrt(pivot[0, 0])
        for i in range(1, 8):
            final = jnp.where(sub == i, rows[i] * lax.rsqrt(pivot[i, i]), final)
        done.append(final)
    return jnp.concatenate(done, axis=0)[:, :n]


def core_kernel(place_ref, mine_ref, other_ref, start_ref, wide_ref, out_ref, gram_ref, full_ref, column_ref, near_ref):
    size = mine_ref.shape[0]
    for part_ref, place in ((mine_ref, place_ref[0]), (other_ref, 1 - place_ref[0])):
        gram_ref[pl.ds(pl.multiple_of(place * size, 8), size), :] = part_ref[...]
    unpack(gram_ref, full_ref)
    dot = functools.partial(
        lax.dot_general, precision=lax.Precision.HIGHEST, preferred_element_type=jnp.float32
    )
    plain, across = (((1,), (0,)), ((), ())), (((1,), (1,)), ((), ()))
    rank = start_ref.shape[0]
    shape = (rank, 2 * rank)
    row, lane = (lax.broadcasted_iota(jnp.int32, shape, axis) for axis in (0, 1))
    eye = (row == lane).astype(jnp.float32)
    image = dot(start_ref[...], full_ref[...], plain)
    for step in range(ITERS):
        small = dot(image, jnp.concatenate([jnp.zeros_like(image), image], axis=0), across)
        follow = dot(image, full_ref[...] if step + 1 < ITERS else wide_ref[...], plain)
        image = dot(inverse_factor(small + eye, column_ref, near_ref), follow, plain)
    out_ref[...] = image


def exchange(x, axes):
    return lax.all_to_all(x, axes, 0, 0, tiled=True)


def added(pieces, count):
    return jnp.sum(pieces.reshape(count, pieces.shape[0] // count, *pieces.shape[1:]), axis=0)


def spread(block, count):
    copies = jnp.broadcast_to(block, (count, *block.shape))
    return copies.reshape(count * block.shape[0], *block.shape[1:])


def shards(count, group_axes, core_axes, plane_axes, line_axes, field, start):
    groups = lax.axis_size(group_axes)
    times, species, rows, planes = field.shape
    moments = times * species
    order, rank = start.shape
    params = pltpu.CompilerParams(vmem_limit_bytes=40 * 1024 * 1024)

    wide = exchange(field.reshape(moments, rows, planes), group_axes)
    wide = wide.reshape(groups, moments // groups, rows, planes)
    wide = jnp.moveaxis(wide, 1, 2).reshape(order, moments // groups * planes)

    depth = depth_of(order)
    cores = lax.axis_size(core_axes)
    half = jax.ShapeDtypeStruct((depth // cores, LANES), jnp.float32)
    place = lax.axis_index(core_axes).astype(jnp.int32).reshape(1)
    scalar = pl.BlockSpec(memory_space=pltpu.SMEM)
    keep, send = pl.pallas_call(
        functools.partial(gram_kernel, 1.0 / count),
        in_specs=[scalar, VMEM],
        out_specs=[VMEM] * 2,
        out_shape=[half] * 2,
        scratch_shapes=[pltpu.VMEM((depth, LANES), jnp.float32)],
        compiler_params=params,
    )(place, wide)

    swap = functools.partial(lax.ppermute, axis_name=core_axes, perm=[(0, 1), (1, 0)])
    gram = (keep + swap(send)).reshape(depth // cores // SLAB, SLAB, LANES)
    gram = added(exchange(gram, plane_axes), lax.axis_size(plane_axes))
    line = lax.axis_size(line_axes)
    gram = added(exchange(spread(gram, line), line_axes), line)
    mine = exchange(spread(gram, lax.axis_size(plane_axes)), plane_axes)
    mine = mine.reshape(depth // cores, LANES)
    other = swap(mine)

    plane_core = pl.pallas_call(
        core_kernel,
        in_specs=[scalar] + [VMEM] * 4,
        out_specs=VMEM,
        out_shape=jax.ShapeDtypeStruct((rank, wide.shape[1]), jnp.float32),
        scratch_shapes=[
            pltpu.VMEM((depth, LANES), jnp.float32),
            pltpu.VMEM((order, order), jnp.float32),
            pltpu.VMEM((rank // 8, 8, 8, 2 * rank), jnp.float32),
            pltpu.VMEM((rank // 8, 8, 8, 2 * rank), jnp.float32),
        ],
        compiler_params=params,
    )(place, mine, other, start.T, wide)
    plane_core = plane_core.reshape(rank, moments // groups, planes)
    plane_core = plane_core.reshape(groups, rank // groups, moments // groups, planes)
    core = exchange(jnp.moveaxis(plane_core, 2, 1).reshape(moments, rank // groups, planes), group_axes)
    return core.reshape(times, species, rank // groups, planes)


def solution(mesh):
    fine = Mesh(
        mesh.devices.reshape(4, 2, 4, 2, 4, 2), ("y", "core", "z_mid", "z_pair", "x", "z_hi")
    )
    placed = P("z_hi", None, ("y", "core"), ("z_mid", "z_pair", "x"))

    def program(field, start):
        count = field.shape[0] * field.shape[1] * field.shape[3]
        body = functools.partial(
            shards,
            count,
            ("y", "core"),
            "core",
            ("y", "z_pair", "x"),
            ("z_mid", "z_hi"),
        )
        return jax.shard_map(
            body, mesh=fine, in_specs=(placed, P()), out_specs=placed, check_vma=False
        )(field, start)

    return program
```

```python
import functools

import jax
import jax.numpy as jnp
from jax import lax
from jax.experimental import pallas as pl
from jax.experimental.pallas import tpu as pltpu
from jax.sharding import Mesh, PartitionSpec as P

ITERS = 2
LANES = 128
HALF = LANES // 2
SLAB = 2
VMEM = pl.BlockSpec(memory_space=pltpu.VMEM)


def split(x):
    high = x.astype(jnp.bfloat16)
    return high, (x - high.astype(jnp.float32)).astype(jnp.bfloat16)


def blocks(order):
    count = order // LANES
    return [(i, j) for i in range(count) for j in range(i + 1, count)]


def depth_of(order):
    return len(blocks(order)) * LANES + order // LANES * HALF * 3 // 2


def gram_kernel(scale, place_ref, wide_ref, keep_ref, send_ref, packed_ref):
    high, low = split(wide_ref[...])
    order = high.shape[0]
    half = order // 2
    dims = (((1,), (1,)), ((), ()))
    dot = functools.partial(lax.dot_general, dimension_numbers=dims, preferred_element_type=jnp.float32)
    parts = {}
    for i in range(2):
        for j in range(i, 2):
            a, b = slice(i * half, (i + 1) * half), slice(j * half, (j + 1) * half)
            mixed = dot(high[a], low[b])
            mirror = mixed.T if i == j else dot(low[a], high[b])
            parts[i, j] = dot(high[a], high[b]) + (mixed + mirror)
    per = half // LANES
    row = 0

    def block(i, j):
        r, c = (i % per) * LANES, (j % per) * LANES
        return parts[i // per, j // per][r : r + LANES, c : c + LANES] * scale

    def store(row, value):
        packed_ref[row : row + value.shape[0], :] = value
        return row + value.shape[0]

    for i, j in blocks(order):
        row = store(row, block(i, j))
    for i in range(0, order // LANES, 2):
        first, second = block(i, i), block(i + 1, i + 1)
        row = store(row, first[:HALF])
        row = store(row, second[:HALF])
        row = store(row, jnp.concatenate([first[HALF:, HALF:], second[HALF:, HALF:]], axis=1))
    size = keep_ref.shape[0]
    for part_ref, place in ((keep_ref, place_ref[0]), (send_ref, 1 - place_ref[0])):
        part_ref[...] = packed_ref[pl.ds(pl.multiple_of(place * size, 8), size), :]


def unpack(gram_ref, full_ref):
    order = full_ref.shape[0]
    row = 0
    for i, j in blocks(order):
        part = gram_ref[row : row + LANES, :]
        full_ref[i * LANES : (i + 1) * LANES, j * LANES : (j + 1) * LANES] = part
        full_ref[j * LANES : (j + 1) * LANES, i * LANES : (i + 1) * LANES] = part.T
        row += LANES
    for i in range(0, order // LANES, 2):
        ends = gram_ref[row + LANES : row + LANES + HALF, :]
        for k in range(2):
            at = (i + k) * LANES
            top = gram_ref[row + k * HALF : row + (k + 1) * HALF, :]
            bottom = [top[:, HALF:].T, ends[:, k * HALF : (k + 1) * HALF]]
            full_ref[at : at + HALF, at : at + LANES] = top
            full_ref[at + HALF : at + LANES, at : at + LANES] = jnp.concatenate(bottom, axis=1)
        row += LANES + HALF


def inverse_factor(work, column_ref, near_ref):
    n = work.shape[0]
    shape = (8, 2 * n)
    panels = n // 8
    tiles = [work[8 * k : 8 * k + 8] for k in range(panels)]
    sub = lax.broadcasted_iota(jnp.int32, shape, 0)
    done = []
    ready = None
    for p in range(panels):
        at = n + 8 * p
        rest = range(p + 1, panels)

        def column(tile, j):
            return jnp.broadcast_to(tile[:, at + j : at + j + 1], shape)

        for j in range(8):
            column_ref[p, j] = column(tiles[p], j) if ready is None else ready[j]
        ready = [column(tiles[p + 1], 8 + j) for j in range(8)] if rest else None
        rows = [jnp.broadcast_to(tiles[p][i : i + 1], shape) for i in range(8)]
        pivot = {
            (i, j): jnp.broadcast_to(column_ref[p, j, i : i + 1, :], shape)
            for j in range(8)
            for i in range(j, 8)
        }
        below = {t: [column(tiles[t], j) for j in range(8)] for t in rest}
        factor, scaled = {}, []
        for i in range(8):
            inverse = 1.0 / pivot[i, i]
            scaled.append(rows[i] * inverse)
            for j in range(i + 1, 8):
                factor[j, i] = pivot[j, i] * inverse
            for j in range(i + 1, 8):
                for m in range(i + 1, j + 1):
                    pivot[j, m] = pivot[j, m] - factor[j, i] * pivot[m, i]
                rows[j] = rows[j] - factor[j, i] * rows[i]
            if rest:
                near_ref[p, i] = below[p + 1][i]
                for j in range(8):
                    across = jnp.broadcast_to(near_ref[p, i, j : j + 1, :], shape)
                    ready[j] = ready[j] - below[p + 1][i] * (across * inverse)
            for t in rest:
                tiles[t] = tiles[t] - below[t][i] * scaled[i]
                for j in range(i + 1, 8):
                    below[t][j] = below[t][j] - factor[j, i] * below[t][i]
        final = rows[0] * lax.rsqrt(pivot[0, 0])
        for i in range(1, 8):
            final = jnp.where(sub == i, rows[i] * lax.rsqrt(pivot[i, i]), final)
        done.append(final)
    return jnp.concatenate(done, axis=0)[:, :n]


def core_kernel(place_ref, mine_ref, other_ref, start_ref, wide_ref, out_ref, gram_ref, full_ref, column_ref, near_ref):
    size = mine_ref.shape[0]
    for part_ref, place in ((mine_ref, place_ref[0]), (other_ref, 1 - place_ref[0])):
        gram_ref[pl.ds(pl.multiple_of(place * size, 8), size), :] = part_ref[...]
    unpack(gram_ref, full_ref)
    dot = functools.partial(
        lax.dot_general, precision=lax.Precision.HIGHEST, preferred_element_type=jnp.float32
    )
    plain, across = (((1,), (0,)), ((), ())), (((1,), (1,)), ((), ()))
    rank = start_ref.shape[0]
    shape = (rank, 2 * rank)
    row, lane = (lax.broadcasted_iota(jnp.int32, shape, axis) for axis in (0, 1))
    eye = (row == lane).astype(jnp.float32)
    image = dot(start_ref[...], full_ref[...], plain)
    for step in range(ITERS):
        small = dot(image, jnp.concatenate([jnp.zeros_like(image), image], axis=0), across)
        follow = dot(image, full_ref[...] if step + 1 < ITERS else wide_ref[...], plain)
        image = dot(inverse_factor(small + eye, column_ref, near_ref), follow, plain)
    out_ref[...] = image


def exchange(x, axes):
    return lax.all_to_all(x, axes, 0, 0, tiled=True)


def added(pieces, count):
    return jnp.sum(pieces.reshape(count, pieces.shape[0] // count, *pieces.shape[1:]), axis=0)


def spread(block, count):
    copies = jnp.broadcast_to(block, (count, *block.shape))
    return copies.reshape(count * block.shape[0], *block.shape[1:])


def shards(count, group_axes, core_axes, plane_axes, line_axes, field, start):
    groups = lax.axis_size(group_axes)
    times, species, rows, planes = field.shape
    moments = times * species
    order, rank = start.shape
    params = pltpu.CompilerParams(vmem_limit_bytes=40 * 1024 * 1024)

    wide = exchange(field.reshape(moments, rows, planes), group_axes)
    wide = wide.reshape(groups, moments // groups, rows, planes)
    wide = jnp.moveaxis(wide, 1, 2).reshape(order, moments // groups * planes)

    depth = depth_of(order)
    cores = lax.axis_size(core_axes)
    half = jax.ShapeDtypeStruct((depth // cores, LANES), jnp.float32)
    place = lax.axis_index(core_axes).astype(jnp.int32).reshape(1)
    scalar = pl.BlockSpec(memory_space=pltpu.SMEM)
    keep, send = pl.pallas_call(
        functools.partial(gram_kernel, 1.0 / count),
        in_specs=[scalar, VMEM],
        out_specs=[VMEM] * 2,
        out_shape=[half] * 2,
        scratch_shapes=[pltpu.VMEM((depth, LANES), jnp.float32)],
        compiler_params=params,
    )(place, wide)

    swap = functools.partial(lax.ppermute, axis_name=core_axes, perm=[(0, 1), (1, 0)])
    gram = (keep + swap(send)).reshape(depth // cores // SLAB, SLAB, LANES)
    gram = added(exchange(gram, plane_axes), lax.axis_size(plane_axes))
    line = lax.axis_size(line_axes)
    gram = added(exchange(spread(gram, line), line_axes), line)
    mine = exchange(spread(gram, lax.axis_size(plane_axes)), plane_axes)
    mine = mine.reshape(depth // cores, LANES)
    other = swap(mine)

    plane_core = pl.pallas_call(
        core_kernel,
        in_specs=[scalar] + [VMEM] * 4,
        out_specs=VMEM,
        out_shape=jax.ShapeDtypeStruct((rank, wide.shape[1]), jnp.float32),
        scratch_shapes=[
            pltpu.VMEM((depth, LANES), jnp.float32),
            pltpu.VMEM((order, order), jnp.float32),
            pltpu.VMEM((rank // 8, 8, 8, 2 * rank), jnp.float32),
            pltpu.VMEM((rank // 8, 8, 8, 2 * rank), jnp.float32),
        ],
        compiler_params=params,
    )(place, mine, other, start.T, wide)
    plane_core = plane_core.reshape(rank, moments // groups, planes)
    plane_core = plane_core.reshape(groups, rank // groups, moments // groups, planes)
    core = exchange(jnp.moveaxis(plane_core, 2, 1).reshape(moments, rank // groups, planes), group_axes)
    return core.reshape(times, species, rank // groups, planes)


def solution(mesh):
    fine = Mesh(
        mesh.devices.reshape(4, 2, 4, 2, 4, 2), ("y", "core", "z_mid", "z_pair", "x", "z_hi")
    )
    placed = P("z_hi", None, ("y", "core"), ("z_mid", "z_pair", "x"))

    def program(field, start):
        count = field.shape[0] * field.shape[1] * field.shape[3]
        body = functools.partial(
            shards,
            count,
            ("y", "core"),
            "core",
            ("x", "z_pair", "y"),
            ("z_mid", "z_hi"),
        )
        return jax.shard_map(
            body, mesh=fine, in_specs=(placed, P()), out_specs=placed, check_vma=False
        )(field, start)

    return program
```
